1024 devices in a mesh: expert: 32 (over x, y), hidden: 32 (over z, core).
Axes of the slice: x: 4, y: 8, z: 16, core: 2. Of those that a mesh axis runs over, the one named last changes fastest.
Arguments:
- tokens: bfloat16 [4096, 4096], P('expert', 'hidden'), may hold values from -6 to 6
- upstream: bfloat16 [4096, 4096], P('expert', 'hidden'), may hold values from -6 to 6
- router: bfloat16 [4096, 32], replicated, may hold values from -0.09375 to 0.09375
- w_gate: bfloat16 [32, 4096, 4096], P('expert', None, 'hidden'), may hold values from -0.09375 to 0.09375
- w_up: bfloat16 [32, 4096, 4096], P('expert', None, 'hidden'), may hold values from -0.09375 to 0.09375
- w_down: bfloat16 [32, 4096, 4096], P('expert', 'hidden'), may hold values from -0.09375 to 0.09375
- chosen: int32 [32, 256], replicated, may hold values from 0 to 4095, as said below
Outputs:
- grad_tokens: bfloat16 [4096, 4096], P('expert', 'hidden')
The draws below stay inside these ranges and needn't reach their ends.
Inputs may be any that keep to these rules, and one draw needn't show every extreme that they name: `chosen`: each row holds 256 distinct token indices. Of one expert's list at most 16 indices lie in one block of 128 consecutive tokens, and every expert has a block with exactly 16.
All inputs are finite; a program needn't handle non-finite values.
Results may differ from the reference program's by a relative error of at most 0.0056.
Values may be sent and summed in bfloat16 or wider, within the bound.
No kernel may reach another device: no remote copies, remote signals or barrier semaphores. Data moves between devices by JAX's collectives and lax.ppermute only.
A program may use at most 32 MiB of HBM per device.

```python
import jax
import jax.numpy as jnp
from jax import lax

D = 4096
FF = 4096
TOK_COL = 128
EXPERTS = 32
TOKENS = 4096
CAP = 256
SLOT = 16


def draw_chosen(key, part):
    key = jax.random.fold_in(key, 11)
    columns = TOKENS // TOK_COL
    half_slot = SLOT // 2
    key_pair, key_move, key_token, key_order = jax.random.split(key, 4)
    pairing = jax.vmap(lambda k: jax.random.permutation(k, columns))(jax.random.split(key_pair, EXPERTS))
    moves = jax.random.randint(key_move, (EXPERTS, columns // 2), 0, half_slot + 1)
    moves = moves.at[:, 0].set(half_slot)
    ordered = jnp.stack([half_slot + moves, half_slot - moves], axis=2).reshape(EXPERTS, columns)
    expert_ids = jnp.arange(EXPERTS, dtype=jnp.int32)[:, None]
    counts = jnp.zeros((EXPERTS, columns), jnp.int32).at[expert_ids, pairing].set(ordered.astype(jnp.int32))
    token_keys = jax.random.split(key_token, EXPERTS * columns)
    within = jax.vmap(lambda k: jax.random.permutation(k, TOK_COL))(token_keys).reshape(EXPERTS, columns, TOK_COL)
    within = within[:, :, :SLOT]
    starts = (jnp.arange(columns, dtype=jnp.int32) * TOK_COL)[None, :, None]
    token_ids = (within + starts).reshape(EXPERTS, columns * SLOT)
    valid = (jnp.arange(SLOT, dtype=jnp.int32)[None, None, :] < counts[:, :, None]).reshape(EXPERTS, columns * SLOT)
    order = jnp.argsort(1 - valid.astype(jnp.int32), axis=1, stable=True)[:, :CAP]
    listed = jnp.take_along_axis(token_ids, order, axis=1)
    shuffle = jax.vmap(lambda k: jax.random.permutation(k, CAP))(jax.random.split(key_order, EXPERTS))
    return jnp.take_along_axis(listed, shuffle, axis=1).astype(jnp.int32)


def levels(own_key, shape, cuts, low, largest):
    def one(dim, blocks):
        heights = jax.random.uniform(jax.random.fold_in(jax.random.fold_in(own_key, 6), dim), (blocks,), jnp.float32, low / len(cuts), largest / len(cuts))
        return jnp.repeat(jnp.exp(heights), shape[dim] // blocks).reshape((-1,) + (1,) * (len(shape) - dim - 1))

    gain = one(*cuts[0])
    for cut in cuts[1:]:
        gain = gain * one(*cut)
    return gain


def gaussian(stream_key, extent, spread, most, shards=(), kind=jnp.bfloat16):
    loudness = levels(stream_key, extent, shards, -0.22, 0.18) if shards else 1.0
    values = jax.random.normal(stream_key, extent, jnp.float32) * spread * loudness
    return jnp.minimum(jnp.maximum(values, -most), most).astype(kind)


def setup_inputs(seed: int = 0) -> dict:
    keys = jax.random.split(jax.random.key(seed), 8)
    return {
        "tokens": gaussian(keys[0], (TOKENS, D), 1.0, 6.0, ((0, 32), (1, 32))),
        "upstream": gaussian(keys[1], (TOKENS, D), 1.0, 6.0, ((0, 32), (1, 32))),
        "router": gaussian(keys[2], (D, EXPERTS), D ** -0.5, 0.09375),
        "w_gate": gaussian(keys[3], (EXPERTS, D, FF), D ** -0.5, 0.09375, ((0, 32), (2, 32))),
        "w_up": gaussian(keys[4], (EXPERTS, D, FF), D ** -0.5, 0.09375, ((0, 32), (2, 32))),
        "w_down": gaussian(keys[5], (EXPERTS, FF, D), FF ** -0.5, 0.09375, ((0, 32), (1, 32))),
        "chosen": draw_chosen(jax.random.fold_in(keys[7], 71), 0),
    }


def per_expert(inputs):
    picked, picked_up, router_col, gate_w, up_w, down_w = inputs
    logit = jnp.dot(picked, router_col, preferred_element_type=jnp.float32)
    weight = jax.nn.sigmoid(logit)
    gate_pre = jnp.dot(picked, gate_w, preferred_element_type=jnp.float32)
    up_pre = jnp.dot(picked, up_w, preferred_element_type=jnp.float32)
    sig = jax.nn.sigmoid(gate_pre)
    act = (gate_pre * sig * up_pre).astype(jnp.bfloat16)
    back_act = jnp.dot(picked_up, down_w.T, preferred_element_type=jnp.float32)
    score_grad = jnp.sum(back_act * act.astype(jnp.float32), axis=1)
    scaled = weight[:, None] * back_act
    d_up = (scaled * gate_pre * sig).astype(jnp.bfloat16)
    d_gate = (scaled * up_pre * sig * (1.0 + gate_pre * (1.0 - sig))).astype(jnp.bfloat16)
    logit_grad = score_grad * weight * (1.0 - weight)
    slot_grad = jnp.dot(d_gate, gate_w.T, preferred_element_type=jnp.float32)
    slot_grad = slot_grad + jnp.dot(d_up, up_w.T, preferred_element_type=jnp.float32)
    slot_grad = slot_grad + logit_grad[:, None] * router_col.astype(jnp.float32)[None, :]
    return slot_grad.astype(jnp.bfloat16)


def reference(tokens, upstream, router, w_gate, w_up, w_down, chosen):
    picked = tokens[chosen]
    picked_up = upstream[chosen]
    slot_grad = lax.map(per_expert, (picked, picked_up, router.T, w_gate, w_up, w_down))
    flat_index = chosen.reshape(-1).astype(jnp.int32)
    total = jnp.zeros(tokens.shape, jnp.float32).at[flat_index].add(slot_grad.reshape(-1, D).astype(jnp.float32))
    return total.astype(jnp.bfloat16)
```

```python
import jax
import jax.numpy as jnp
from jax import lax
from jax.experimental import pallas as pl
from jax.experimental.pallas import tpu as pltpu
from jax.sharding import PartitionSpec as P

F32 = jnp.float32
BF16 = jnp.bfloat16
SLOT = 16
VMEM_LIMIT = 56 * 1024 * 1024
LAST = (((1,), (1,)), ((), ()))
FIRST = (((0,), (0,)), ((), ()))
STEPS = (64, 16, 8, 4, 2, 1)
BASE = 13


def mm(a, b, dims=(((1,), (0,)), ((), ()))):
    return lax.dot_general(a, b, dims, preferred_element_type=F32)


def call(kernel, out, *args, flops=0, ids=None):
    specs = [pl.BlockSpec(memory_space=pltpu.VMEM)] * len(args)
    if ids is not None:
        specs = [pl.BlockSpec(memory_space=pltpu.SMEM)] + specs
        args = (ids,) + args
    moved = sum(a.size * a.dtype.itemsize for a in args) + sum(o.size * o.dtype.itemsize for o in out)
    return pl.pallas_call(
        kernel,
        out_shape=list(out),
        in_specs=specs,
        out_specs=[pl.BlockSpec(memory_space=pltpu.VMEM)] * len(out),
        compiler_params=pltpu.CompilerParams(vmem_limit_bytes=VMEM_LIMIT),
        cost_estimate=pl.CostEstimate(flops=flops, bytes_accessed=moved, transcendentals=0),
    )(*args)


def shape(dims, dtype):
    return jax.ShapeDtypeStruct(dims, dtype)


def iota(dims, axis):
    return lax.broadcasted_iota(jnp.int32, dims, axis)


def route_kernel(ids, chosen_ref, tok_ref, up_ref, blocks_ref, sender_ref, packer_ref):
    col = ids[0]
    experts, cap = chosen_ref.shape
    count = tok_ref.shape[0]
    slots = experts * SLOT
    token = iota((count, cap), 0) + col * count
    lane = iota((count, experts), 1)
    mask = jnp.zeros((count, experts), F32)
    for e in range(experts):
        hit = jnp.sum((chosen_ref[e : e + 1, :] == token).astype(F32), axis=1, keepdims=True)
        mask = jnp.where(lane == e, hit, mask)
    mask = mask.astype(BF16)
    earlier = (iota((count, count), 0) > iota((count, count), 1)).astype(F32).astype(BF16)
    rank = mm(earlier, mask).astype(BF16)
    spread = (iota((experts, slots), 1) // SLOT == iota((experts, slots), 0)).astype(F32).astype(BF16)
    place = (iota((count, slots), 1) % SLOT).astype(F32)
    sender = jnp.logical_and(mm(mask, spread) > 0.5, mm(rank, spread) == place).astype(F32).astype(BF16)
    sender_ref[...] = sender
    blocks_ref[...] = mm(sender, jnp.concatenate([tok_ref[...], up_ref[...]], axis=1), FIRST).astype(BF16)
    own = chosen_ref[pl.ds(col, 1), :] // count
    block = iota((slots, cap), 0) // SLOT
    held = jnp.sum((own == block).astype(F32), axis=1, keepdims=True)
    before = jnp.sum((own < block).astype(F32), axis=1, keepdims=True)
    place = (iota((slots, 1), 0) % SLOT).astype(F32)
    row = jnp.where(place < held, before + place, -1.0)
    packer_ref[...] = (row == iota((slots, cap), 1).astype(F32)).astype(F32).astype(BF16)


def scale_up(rows):
    top = jnp.max(jnp.max(jnp.abs(rows), axis=1, keepdims=True), axis=0, keepdims=True)
    power = jnp.zeros_like(top)
    factor = jnp.full_like(top, 2.0**BASE)
    for step in STEPS:
        small = top <= 2.0 ** (2 - step)
        top = jnp.where(small, top * 2.0**step, top)
        factor = jnp.where(small, factor * 2.0**step, factor)
        power = jnp.where(small, power + step, power)
    return rows * factor, power


def pack_kernel(arrived_ref, packer_ref, out_ref):
    cap = packer_ref.shape[1]
    half = arrived_ref.shape[1] // 2
    rows = mm(packer_ref[...], arrived_ref[...], FIRST)
    for part in range(2):
        lanes = slice(part * half, (part + 1) * half)
        scaled, power = scale_up(rows[:, lanes])
        out_ref[:cap, lanes] = scaled
        out_ref[cap:, lanes] = jnp.broadcast_to(power, (out_ref.shape[0] - cap, half))


def expert_kernel(ids, x_ref, gate_ref, up_ref, down_ref, router_ref, own_ref, sib_ref):
    col, core, parity = ids[0], ids[1], ids[2]
    chips = x_ref.shape[0] // 2
    rows = x_ref.shape[1]
    width = gate_ref.shape[1]
    experts = router_ref.shape[1]
    pre = jnp.zeros((rows, 2 * width), F32)
    back = jnp.zeros((rows, width), F32)
    logit = jnp.zeros((rows, experts), F32)
    for j in range(chips):
        at = slice(2 * j * width, 2 * (j + 1) * width)
        x = jnp.concatenate([x_ref[2 * j, :, :width], x_ref[2 * j + 1, :, :width]], axis=1)
        u = jnp.concatenate([x_ref[2 * j, :, width:], x_ref[2 * j + 1, :, width:]], axis=1)
        pre += mm(x, jnp.concatenate([gate_ref[at, :], up_ref[at, :]], axis=1))
        back += mm(u, down_ref[:, at], LAST)
        logit += mm(x, router_ref[at, :])
    logit = jnp.sum(jnp.where(iota((rows, experts), 1) == col, logit, 0.0), axis=1, keepdims=True)
    weight = 1.0 / (1.0 + jnp.exp(-logit))
    gate_pre, up_pre = pre[:, :width], pre[:, width:]
    sig = 1.0 / (1.0 + jnp.exp(-gate_pre))
    act = (gate_pre * sig * up_pre).astype(BF16)
    score = jnp.sum(back * act.astype(F32), axis=1, keepdims=True)
    scaled = weight * back
    d_up = (scaled * gate_pre * sig).astype(BF16)
    d_gate = (scaled * up_pre * sig * (1.0 + gate_pre * (1.0 - sig))).astype(BF16)
    grads = jnp.concatenate([d_gate, d_up], axis=1)
    slope = score * (weight * (1.0 - weight))
    pick = (iota((8, experts), 1) == col).astype(F32).astype(BF16)
    for j in range(chips):
        at = slice(2 * j * width, 2 * (j + 1) * width)
        terms = mm(grads, jnp.concatenate([gate_ref[at, :], up_ref[at, :]], axis=1), LAST)
        terms += slope * mm(pick, router_ref[at, :], LAST)[:1, :]
        low, high = terms[:, :width], terms[:, width:]
        place = j // 2 + jnp.where(parity == j % 2, chips // 2, 0)
        own_ref[place] = jnp.where(core == 0, low, high)
        sib_ref[place] = jnp.where(core == 0, high, low).astype(BF16)


def pair_kernel(own_ref, arrived_ref, up_ref, down_ref, keep_ref):
    half = up_ref.shape[0]
    mid = up_ref.shape[1]
    up_ref[...] = (own_ref[:half, :mid] + arrived_ref[:half, :mid].astype(F32)).astype(BF16)
    down_ref[...] = (own_ref[:half, mid:] + arrived_ref[:half, mid:].astype(F32)).astype(BF16)
    keep_ref[...] = own_ref[half:] + arrived_ref[half:].astype(F32)


def near_kernel(keep_ref, low_ref, high_ref, out_ref):
    mid = low_ref.shape[1]
    out_ref[:, :mid] = (keep_ref[:, :mid] + low_ref[...].astype(F32)).astype(BF16)
    out_ref[:, mid:] = (keep_ref[:, mid:] + high_ref[...].astype(F32)).astype(BF16)


def unpack_kernel(parts_ref, packer_ref, out_ref):
    total = parts_ref[0].astype(F32)
    for i in range(1, parts_ref.shape[0]):
        total += parts_ref[i].astype(F32)
    out_ref[...] = mm(packer_ref[...], total.astype(BF16)).astype(BF16)


def gather_kernel(sender_ref, arrived_ref, out_ref):
    out_ref[...] = mm(sender_ref[...], arrived_ref[...]).astype(BF16)


def body(tokens, upstream, router, w_gate, w_up, w_down, chosen):
    experts = lax.axis_size("expert")
    devices = lax.axis_size("hidden")
    chips = devices // 2
    expert_id = lax.axis_index("expert")
    hidden_id = lax.axis_index("hidden")
    count, width = tokens.shape
    cap = chosen.shape[1]
    slots = experts * SLOT
    ids = jnp.stack([expert_id, hidden_id % 2, (hidden_id // 2) % 2]).astype(jnp.int32)

    blocks, sender, packer = call(
        route_kernel,
        [shape((slots, 2 * width), BF16), shape((count, slots), BF16), shape((slots, cap), BF16)],
        chosen, tokens, upstream, ids=ids,
    )
    arrived = lax.all_to_all(blocks.reshape(experts, SLOT, 2 * width), "expert", 0, 0, tiled=True)
    (rows,) = call(pack_kernel, [shape((cap + 16, 2 * width), F32)], arrived.reshape(slots, 2 * width), packer)
    full = lax.all_gather(rows.astype(jnp.float16), "hidden", axis=0)
    undo = jnp.exp2(-(full[:, cap : cap + 1, :].astype(F32) + BASE))
    picked = (full[:, :cap, :].astype(F32) * undo).astype(BF16)

    own, sibling = call(
        expert_kernel,
        [shape((chips, cap, width), F32), shape((chips, cap, width), BF16)],
        picked, w_gate[0], w_up[0], w_down[0], router,
        ids=ids, flops=10 * cap * devices * width * width,
    )
    arrived = lax.ppermute(sibling, "hidden", [(i, i ^ 1) for i in range(devices)])
    half = chips // 2
    mid = cap // 2
    up, down, keep = call(
        pair_kernel,
        [shape((half, mid, width), BF16), shape((half, mid, width), BF16), shape((half, cap, width), F32)],
        own, arrived,
    )
    low = lax.ppermute(up, "hidden", [(i, (i + 2) % devices) for i in range(devices)])
    high = lax.ppermute(down, "hidden", [(i, (i - 2) % devices) for i in range(devices)])
    (near,) = call(near_kernel, [shape((half, cap, width), BF16)], keep, low, high)
    groups = [[c + 2 * p + 4 * r for r in range(half)] for p in range(2) for c in range(2)]
    parts = lax.all_to_all(near, "hidden", 0, 0, tiled=True, axis_index_groups=groups)
    (outgoing,) = call(unpack_kernel, [shape((slots, width), BF16)], parts, packer)
    arrived = lax.all_to_all(outgoing.reshape(experts, SLOT, width), "expert", 0, 0, tiled=True)
    (grad,) = call(gather_kernel, [shape((count, width), BF16)], sender, arrived.reshape(slots, width))
    return grad


def solution(mesh):
    in_specs = (
        P("expert", "hidden"),
        P("expert", "hidden"),
        P(),
        P("expert", None, "hidden"),
        P("expert", None, "hidden"),
        P("expert", "hidden", None),
        P(),
    )
    out_specs = P("expert", "hidden")
    return jax.shard_map(body, mesh=mesh, in_specs=in_specs, out_specs=out_specs, check_vma=False)
```

```python
import jax
import jax.numpy as jnp
from jax import lax
from jax.experimental import pallas as pl
from jax.experimental.pallas import tpu as pltpu
from jax.sharding import PartitionSpec as P

F32 = jnp.float32
BF16 = jnp.bfloat16
SLOT = 16
LAST = (((1,), (1,)), ((), ()))
FIRST = (((0,), (0,)), ((), ()))
STEPS = (64, 16, 8, 4, 2, 1)
BASE = 13


def mm(a, b, dims=(((1,), (0,)), ((), ()))):
    return lax.dot_general(a, b, dims, preferred_element_type=F32)


def call(kernel, out, *args, flops=0, vmem=16, stream=False, scratch=()):
    spec = pl.BlockSpec(memory_space=pl.ANY if stream else pltpu.VMEM)
    moved = sum(a.size * a.dtype.itemsize for a in args) + sum(o.size * o.dtype.itemsize for o in out)
    return pl.pallas_call(
        kernel,
        out_shape=list(out),
        in_specs=[spec] * len(args),
        out_specs=[spec] * len(out),
        scratch_shapes=list(scratch),
        compiler_params=pltpu.CompilerParams(vmem_limit_bytes=vmem * 1024 * 1024),
        cost_estimate=pl.CostEstimate(flops=flops, bytes_accessed=moved, transcendentals=0),
    )(*args)


def shape(dims, dtype):
    return jax.ShapeDtypeStruct(dims, dtype)


def iota(dims, axis):
    return lax.broadcasted_iota(jnp.int32, dims, axis)


def route_kernel(chosen_ref, tok_ref, up_ref, blocks_ref, sender_ref, packer_ref):
    col = lax.axis_index("expert")
    experts, cap = chosen_ref.shape
    count = tok_ref.shape[0]
    slots = experts * SLOT
    token = iota((count, cap), 0) + col * count
    lane = iota((count, experts), 1)
    mask = jnp.zeros((count, experts), F32)
    for e in range(experts):
        hit = jnp.sum((chosen_ref[e : e + 1, :] == token).astype(F32), axis=1, keepdims=True)
        mask = jnp.where(lane == e, hit, mask)
    mask = mask.astype(BF16)
    earlier = (iota((count, count), 0) > iota((count, count), 1)).astype(F32).astype(BF16)
    rank = mm(earlier, mask).astype(BF16)
    spread = (iota((experts, slots), 1) // SLOT == iota((experts, slots), 0)).astype(F32).astype(BF16)
    place = (iota((count, slots), 1) % SLOT).astype(F32)
    sender = jnp.logical_and(mm(mask, spread) > 0.5, mm(rank, spread) == place).astype(F32).astype(BF16)
    sender_ref[...] = sender
    blocks_ref[...] = mm(sender, jnp.concatenate([tok_ref[...], up_ref[...]], axis=1), FIRST).astype(BF16)
    own = chosen_ref[pl.ds(col, 1), :] // count
    block = iota((slots, cap), 0) // SLOT
    held = jnp.sum((own == block).astype(F32), axis=1, keepdims=True)
    before = jnp.sum((own < block).astype(F32), axis=1, keepdims=True)
    place = (iota((slots, 1), 0) % SLOT).astype(F32)
    row = jnp.where(place < held, before + place, -1.0)
    packer_ref[...] = (row == iota((slots, cap), 1).astype(F32)).astype(F32).astype(BF16)


def scale_up(rows):
    top = jnp.max(jnp.max(jnp.abs(rows), axis=1, keepdims=True), axis=0, keepdims=True)
    power = jnp.zeros_like(top)
    factor = jnp.full_like(top, 2.0**BASE)
    for step in STEPS:
        small = top <= 2.0 ** (2 - step)
        top = jnp.where(small, top * 2.0**step, top)
        factor = jnp.where(small, factor * 2.0**step, factor)
        power = jnp.where(small, power + step, power)
    return rows * factor, power


def pack_kernel(arrived_ref, packer_ref, out_ref):
    cap = packer_ref.shape[1]
    half = arrived_ref.shape[1] // 2
    rows = mm(packer_ref[...], arrived_ref[...], FIRST)
    for part in range(2):
        lanes = slice(part * half, (part + 1) * half)
        scaled, power = scale_up(rows[:, lanes])
        out_ref[:cap, lanes] = scaled.astype(BF16)
        out_ref[cap:, lanes] = jnp.broadcast_to(power, (out_ref.shape[0] - cap, half)).astype(BF16)


def expert_kernel(
    x_hbm, gate_hbm, up_hbm, down_hbm, router_hbm, own_hbm, sib_hbm,
    x_ref, gate_ref, up_ref, down_ref, router_ref, own_ref, sib_ref, in_sem, router_sem, out_sem,
):
    col = lax.axis_index("expert")
    hidden = lax.axis_index("hidden")
    core, chip = hidden % 2, hidden // 2
    chips = x_ref.shape[0] // 2
    rows = x_ref.shape[1]
    width = gate_ref.shape[1]

    def span(j):
        return pl.ds(2 * j * width, 2 * width)

    def loads(j):
        pairs = (
            (x_hbm.at[pl.ds(2 * j, 2)], x_ref.at[pl.ds(2 * j, 2)]),
            (gate_hbm.at[span(j), :], gate_ref.at[span(j), :]),
            (up_hbm.at[span(j), :], up_ref.at[span(j), :]),
            (down_hbm.at[:, span(j)], down_ref.at[:, span(j)]),
        )
        return [pltpu.make_async_copy(a, b, in_sem.at[j, i]) for i, (a, b) in enumerate(pairs)]

    router_load = pltpu.make_async_copy(router_hbm, router_ref, router_sem.at[0])
    router_load.start()
    for j in range(chips):
        for copy in loads(j):
            copy.start()
    router_load.wait()
    picks = iota(router_ref.shape, 0) == col
    router = jnp.sum(jnp.where(picks, router_ref[...].astype(F32), 0.0), axis=0, keepdims=True)

    def at(j):
        return slice(2 * j * width, 2 * (j + 1) * width)

    pre = jnp.zeros((rows, 2 * width), F32)
    back = jnp.zeros((rows, width), F32)
    logit = jnp.zeros((rows, width), F32)
    for j in range(chips):
        for copy in loads(j):
            copy.wait()
        x = jnp.concatenate([x_ref[2 * j, :, :width], x_ref[2 * j + 1, :, :width]], axis=1)
        u = jnp.concatenate([x_ref[2 * j, :, width:], x_ref[2 * j + 1, :, width:]], axis=1)
        pre += mm(x, jnp.concatenate([gate_ref[at(j), :], up_ref[at(j), :]], axis=1))
        back += mm(u, down_ref[:, at(j)], LAST)
        logged = x.astype(F32) * router[:, at(j)]
        logit += logged[:, :width] + logged[:, width:]
    logit = jnp.sum(logit, axis=1, keepdims=True)
    weight = 1.0 / (1.0 + jnp.exp(-logit))
    gate_pre, up_pre = pre[:, :width], pre[:, width:]
    sig = 1.0 / (1.0 + jnp.exp(-gate_pre))
    act = (gate_pre * sig * up_pre).astype(BF16)
    score = jnp.sum(back * act.astype(F32), axis=1, keepdims=True)
    scaled = weight * back
    d_up = (scaled * gate_pre * sig).astype(BF16)
    d_gate = (scaled * up_pre * sig * (1.0 + gate_pre * (1.0 - sig))).astype(BF16)
    grads = jnp.concatenate([d_gate, d_up], axis=1)
    slope = score * (weight * (1.0 - weight))

    def stores(j, place):
        pairs = ((sib_ref.at[j], sib_hbm.at[place]), (own_ref.at[j], own_hbm.at[place]))
        return [pltpu.make_async_copy(a, b, out_sem.at[j, i]) for i, (a, b) in enumerate(pairs)]

    for j in range(chips):
        terms = mm(grads, jnp.concatenate([gate_ref[at(j), :], up_ref[at(j), :]], axis=1), LAST)
        terms += slope * router[:, at(j)]
        low, high = terms[:, :width], terms[:, width:]
        own_ref[j] = jnp.where(core == 0, low, high)
        sib_ref[j] = jnp.where(core == 0, high, low).astype(BF16)
        for copy in stores(j, (j + chips - chip) % 4 * (chips // 4) + j // 4):
            copy.start()
    for j in range(chips):
        for copy in stores(j, 0):
            copy.wait()


def body(tokens, upstream, router, w_gate, w_up, w_down, chosen):
    experts = lax.axis_size("expert")
    devices = lax.axis_size("hidden")
    chips = devices // 2
    count, width = tokens.shape
    cap = chosen.shape[1]
    slots = experts * SLOT

    blocks, sender, packer = call(
        route_kernel,
        [shape((slots, 2 * width), BF16), shape((count, slots), BF16), shape((slots, cap), BF16)],
        chosen, tokens, upstream,
    )
    arrived = lax.all_to_all(blocks.reshape(experts, SLOT, 2 * width), "expert", 0, 0, tiled=True)
    (rows,) = call(pack_kernel, [shape((cap + 16, 2 * width), BF16)], arrived.reshape(slots, 2 * width), packer)
    full = lax.all_gather(rows.astype(jnp.float16), "hidden", axis=0)
    undo = jnp.exp2(-(full[:, cap : cap + 1, :].astype(F32) + BASE))
    picked = (full[:, :cap, :].astype(F32) * undo).astype(BF16)

    own, sibling = call(
        expert_kernel,
        [shape((chips, cap, width), F32), shape((chips, cap, width), BF16)],
        picked, w_gate[0], w_up[0], w_down[0], router.T,
        flops=10 * cap * devices * width * width,
        vmem=24,
        stream=True,
        scratch=[
            pltpu.VMEM(picked.shape, BF16),
            pltpu.VMEM(w_gate.shape[1:], BF16),
            pltpu.VMEM(w_up.shape[1:], BF16),
            pltpu.VMEM(w_down.shape[1:], BF16),
            pltpu.VMEM(router.shape[::-1], BF16),
            pltpu.VMEM((chips, cap, width), F32),
            pltpu.VMEM((chips, cap, width), BF16),
            pltpu.SemaphoreType.DMA((chips, 4)),
            pltpu.SemaphoreType.DMA((1,)),
            pltpu.SemaphoreType.DMA((chips, 2)),
        ],
    )

    def shift(v, hops):
        return lax.ppermute(v, "hidden", [(i, (i + 2 * hops) % devices) for i in range(devices)])

    arrived = lax.ppermute(sibling, "hidden", [(i, i ^ 1) for i in range(devices)])
    part = chips // 4
    mid = cap // 2

    def both(group, lines):
        at = slice(group * part, (group + 1) * part)
        return own[at, lines] + arrived[at, lines].astype(F32)

    every = slice(0, cap)
    two_up = shift(both(2, slice(0, mid)).astype(BF16), 2)
    two_down = shift(both(2, slice(mid, cap)).astype(BF16), -2)
    one_up = shift(both(1, every).astype(BF16), 1)
    one_down = shift(both(3, every).astype(BF16), -1)
    two = jnp.concatenate([two_up, two_down], axis=1).astype(F32)
    near = (both(0, every) + one_up.astype(F32) + one_down.astype(F32) + two).astype(BF16)
    groups = [[c + 2 * q + 8 * r for r in range(part)] for q in range(4) for c in range(2)]
    parts = lax.all_to_all(near, "hidden", 0, 0, tiled=True, axis_index_groups=groups)
    slot_grad = jnp.sum(parts.astype(F32), axis=0).astype(BF16)
    outgoing = mm(packer, slot_grad).astype(BF16)
    arrived = lax.all_to_all(outgoing.reshape(experts, SLOT, width), "expert", 0, 0, tiled=True)
    return mm(sender, arrived.reshape(slots, width)).astype(BF16)


def solution(mesh):
    in_specs = (
        P("expert", "hidden"),
        P("expert", "hidden"),
        P(),
        P("expert", None, "hidden"),
        P("expert", None, "hidden"),
        P("expert", "hidden", None),
        P(),
    )
    out_specs = P("expert", "hidden")
    return jax.shard_map(body, mesh=mesh, in_specs=in_specs, out_specs=out_specs, check_vma=False)
```

```python
import jax
import jax.numpy as jnp
from jax import lax
from jax.experimental import pallas as pl
from jax.experimental.pallas import tpu as pltpu
from jax.sharding import PartitionSpec as P

F32 = jnp.float32
BF16 = jnp.bfloat16
SLOT = 16
LAST = (((1,), (1,)), ((), ()))
FIRST = (((0,), (0,)), ((), ()))
STEPS = (64, 16, 8, 4, 2, 1)
BASE = 13


def mm(a, b, dims=(((1,), (0,)), ((), ()))):
    return lax.dot_general(a, b, dims, preferred_element_type=F32)


def call(kernel, out, *args, flops=0, vmem=16, stream=False, scratch=()):
    spec = pl.BlockSpec(memory_space=pltpu.VMEM)
    moved = sum(a.size * a.dtype.itemsize for a in args) + sum(o.size * o.dtype.itemsize for o in out)
    return pl.pallas_call(
        kernel,
        out_shape=list(out),
        in_specs=[pl.BlockSpec(memory_space=pltpu.HBM) if stream else spec] * len(args),
        out_specs=[spec] * len(out),
        scratch_shapes=list(scratch),
        compiler_params=pltpu.CompilerParams(vmem_limit_bytes=vmem * 1024 * 1024),
        cost_estimate=pl.CostEstimate(flops=flops, bytes_accessed=moved, transcendentals=0),
    )(*args)


def shape(dims, dtype):
    return jax.ShapeDtypeStruct(dims, dtype)


def iota(dims, axis):
    return lax.broadcasted_iota(jnp.int32, dims, axis)


def route_kernel(chosen_hbm, tok_hbm, up_hbm, blocks_ref, sender_ref, packer_ref, chosen_ref, tok_ref, up_ref, sem):
    pairs = ((chosen_hbm, chosen_ref), (tok_hbm, tok_ref), (up_hbm, up_ref))
    loads = [pltpu.make_async_copy(a, b, sem.at[i]) for i, (a, b) in enumerate(pairs)]
    for load in loads:
        load.start()
    loads[0].wait()
    col = lax.axis_index("expert")
    experts, cap = chosen_ref.shape
    count = tok_ref.shape[0]
    slots = experts * SLOT
    token = iota((count, cap), 0) + col * count
    lane = iota((count, experts), 1)
    mask = jnp.zeros((count, experts), F32)
    for e in range(experts):
        hit = jnp.sum((chosen_ref[e : e + 1, :] == token).astype(F32), axis=1, keepdims=True)
        mask = jnp.where(lane == e, hit, mask)
    mask = mask.astype(BF16)
    earlier = (iota((count, count), 0) > iota((count, count), 1)).astype(F32).astype(BF16)
    rank = mm(earlier, mask).astype(BF16)
    spread = (iota((experts, slots), 1) // SLOT == iota((experts, slots), 0)).astype(F32).astype(BF16)
    place = (iota((count, slots), 1) % SLOT).astype(F32)
    sender = jnp.logical_and(mm(mask, spread) > 0.5, mm(rank, spread) == place).astype(F32).astype(BF16)
    sender_ref[...] = sender
    loads[1].wait()
    loads[2].wait()
    blocks_ref[...] = mm(sender, jnp.concatenate([tok_ref[...], up_ref[...]], axis=1), FIRST).astype(BF16)
    own = chosen_ref[pl.ds(col, 1), :] // count
    block = iota((slots, cap), 0) // SLOT
    held = jnp.sum((own == block).astype(F32), axis=1, keepdims=True)
    before = jnp.sum((own < block).astype(F32), axis=1, keepdims=True)
    place = (iota((slots, 1), 0) % SLOT).astype(F32)
    row = jnp.where(place < held, before + place, -1.0)
    packer_ref[...] = (row == iota((slots, cap), 1).astype(F32)).astype(F32).astype(BF16)


def scale_up(rows):
    top = jnp.max(jnp.max(jnp.abs(rows), axis=1, keepdims=True), axis=0, keepdims=True)
    power = jnp.zeros_like(top)
    factor = jnp.full_like(top, 2.0**BASE)
    for step in STEPS:
        small = top <= 2.0 ** (2 - step)
        top = jnp.where(small, top * 2.0**step, top)
        factor = jnp.where(small, factor * 2.0**step, factor)
        power = jnp.where(small, power + step, power)
    return rows * factor, power


def pack_kernel(arrived_ref, packer_ref, out_ref):
    cap = packer_ref.shape[1]
    half = arrived_ref.shape[1] // 2
    rows = mm(packer_ref[...], arrived_ref[...], FIRST)
    for part in range(2):
        lanes = slice(part * half, (part + 1) * half)
        scaled, power = scale_up(rows[:, lanes])
        out_ref[:cap, lanes] = scaled.astype(BF16)
        out_ref[cap:, lanes] = jnp.broadcast_to(power, (out_ref.shape[0] - cap, half)).astype(BF16)


def expert_kernel(x_ref, gate_ref, up_ref, down_ref, router_ref, own_ref, sib_ref):
    col = lax.axis_index("expert")
    hidden = lax.axis_index("hidden")
    core, chip = hidden % 2, hidden // 2
    chips = x_ref.shape[0] // 2
    rows = x_ref.shape[1]
    width = gate_ref.shape[1]
    picks = iota(router_ref.shape, 0) == col
    router = jnp.sum(jnp.where(picks, router_ref[...].astype(F32), 0.0), axis=0, keepdims=True)

    def at(j):
        return slice(2 * j * width, 2 * (j + 1) * width)

    pre = jnp.zeros((rows, 2 * width), F32)
    back = jnp.zeros((rows, width), F32)
    logit = jnp.zeros((rows, width), F32)
    for j in range(chips):
        x = jnp.concatenate([x_ref[2 * j, :, :width], x_ref[2 * j + 1, :, :width]], axis=1)
        u = jnp.concatenate([x_ref[2 * j, :, width:], x_ref[2 * j + 1, :, width:]], axis=1)
        pre += mm(x, jnp.concatenate([gate_ref[at(j), :], up_ref[at(j), :]], axis=1))
        back += mm(u, down_ref[:, at(j)], LAST)
        logged = x.astype(F32) * router[:, at(j)]
        logit += logged[:, :width] + logged[:, width:]
    logit = jnp.sum(logit, axis=1, keepdims=True)
    weight = 1.0 / (1.0 + jnp.exp(-logit))
    gate_pre, up_pre = pre[:, :width], pre[:, width:]
    sig = 1.0 / (1.0 + jnp.exp(-gate_pre))
    act = (gate_pre * sig * up_pre).astype(BF16)
    score = jnp.sum(back * act.astype(F32), axis=1, keepdims=True)
    scaled = weight * back
    d_up = (scaled * gate_pre * sig).astype(BF16)
    d_gate = (scaled * up_pre * sig * (1.0 + gate_pre * (1.0 - sig))).astype(BF16)
    grads = jnp.concatenate([d_gate, d_up], axis=1)
    slope = score * (weight * (1.0 - weight))

    for j in range(chips):
        terms = mm(grads, jnp.concatenate([gate_ref[at(j), :], up_ref[at(j), :]], axis=1), LAST)
        terms += slope * router[:, at(j)]
        low, high = terms[:, :width], terms[:, width:]
        place = (j + chips - chip) % 4 * (chips // 4) + j // 4
        own_ref[place] = jnp.where(core == 0, low, high)
        sib_ref[place] = jnp.where(core == 0, high, low).astype(BF16)


def body(tokens, upstream, router, w_gate, w_up, w_down, chosen):
    experts = lax.axis_size("expert")
    devices = lax.axis_size("hidden")
    chips = devices // 2
    count, width = tokens.shape
    cap = chosen.shape[1]
    slots = experts * SLOT

    blocks, sender, packer = call(
        route_kernel,
        [shape((slots, 2 * width), BF16), shape((count, slots), BF16), shape((slots, cap), BF16)],
        chosen, tokens, upstream,
        stream=True,
        scratch=[
            pltpu.VMEM(chosen.shape, jnp.int32),
            pltpu.VMEM(tokens.shape, BF16),
            pltpu.VMEM(upstream.shape, BF16),
            pltpu.SemaphoreType.DMA((3,)),
        ],
    )
    arrived = lax.all_to_all(blocks.reshape(experts, SLOT, 2 * width), "expert", 0, 0, tiled=True)
    (rows,) = call(pack_kernel, [shape((cap + 16, 2 * width), BF16)], arrived.reshape(slots, 2 * width), packer)
    full = lax.all_gather(rows.astype(jnp.float16), "hidden", axis=0)
    undo = jnp.exp2(-(full[:, cap : cap + 1, :].astype(F32) + BASE))
    picked = (full[:, :cap, :].astype(F32) * undo).astype(BF16)

    own, sibling = call(
        expert_kernel,
        [shape((chips, cap, width), F32), shape((chips, cap, width), BF16)],
        picked, w_gate[0], w_up[0], w_down[0], router.T,
        flops=10 * cap * devices * width * width,
        vmem=24,
    )

    def shift(v, hops):
        return lax.ppermute(v, "hidden", [(i, (i + 2 * hops) % devices) for i in range(devices)])

    arrived = lax.ppermute(sibling, "hidden", [(i, i ^ 1) for i in range(devices)])
    part = chips // 4
    mid = cap // 2

    def both(group, lines):
        at = slice(group * part, (group + 1) * part)
        return own[at, lines] + arrived[at, lines].astype(F32)

    every = slice(0, cap)
    two_up = shift(both(2, slice(0, mid)).astype(BF16), 2)
    two_down = shift(both(2, slice(mid, cap)).astype(BF16), -2)
    one_up = shift(both(1, every).astype(BF16), 1)
    one_down = shift(both(3, every).astype(BF16), -1)
    two = jnp.concatenate([two_up, two_down], axis=1).astype(F32)
    near = (both(0, every) + one_up.astype(F32) + one_down.astype(F32) + two).astype(BF16)
    groups = [[c + 2 * q + 8 * r for r in range(part)] for q in range(4) for c in range(2)]
    parts = lax.all_to_all(near, "hidden", 0, 0, tiled=True, axis_index_groups=groups)
    slot_grad = jnp.sum(parts.astype(F32), axis=0).astype(BF16)
    outgoing = mm(packer, slot_grad).astype(BF16)
    arrived = lax.all_to_all(outgoing.reshape(experts, SLOT, width), "expert", 0, 0, tiled=True)
    return mm(sender, arrived.reshape(slots, width)).astype(BF16)


def solution(mesh):
    in_specs = (
        P("expert", "hidden"),
        P("expert", "hidden"),
        P(),
        P("expert", None, "hidden"),
        P("expert", None, "hidden"),
        P("expert", "hidden", None),
        P(),
    )
    out_specs = P("expert", "hidden")
    return jax.shard_map(body, mesh=mesh, in_specs=in_specs, out_specs=out_specs, check_vma=False)
```

```python
import jax
import jax.numpy as jnp
from jax import lax
from jax.experimental import pallas as pl
from jax.experimental.pallas import tpu as pltpu
from jax.sharding import PartitionSpec as P

F32 = jnp.float32
BF16 = jnp.bfloat16
SLOT = 16
LAST = (((1,), (1,)), ((), ()))
FIRST = (((0,), (0,)), ((), ()))
STEPS = (64, 16, 8, 4, 2, 1)
BASE = 13


def mm(a, b, dims=(((1,), (0,)), ((), ()))):
    return lax.dot_general(a, b, dims, preferred_element_type=F32)


def call(kernel, out, *args, flops=0, vmem=16, stream=False, scratch=()):
    spec = pl.BlockSpec(memory_space=pltpu.VMEM)
    moved = sum(a.size * a.dtype.itemsize for a in args) + sum(o.size * o.dtype.itemsize for o in out)
    return pl.pallas_call(
        kernel,
        out_shape=list(out),
        in_specs=[pl.BlockSpec(memory_space=pltpu.HBM) if stream else spec] * len(args),
        out_specs=[spec] * len(out),
        scratch_shapes=list(scratch),
        compiler_params=pltpu.CompilerParams(vmem_limit_bytes=vmem * 1024 * 1024),
        cost_estimate=pl.CostEstimate(flops=flops, bytes_accessed=moved, transcendentals=0),
    )(*args)


def shape(dims, dtype):
    return jax.ShapeDtypeStruct(dims, dtype)


def iota(dims, axis):
    return lax.broadcasted_iota(jnp.int32, dims, axis)


def route_kernel(chosen_hbm, tok_hbm, up_hbm, blocks_ref, sender_ref, packer_ref, chosen_ref, tok_ref, up_ref, sem):
    pairs = ((chosen_hbm, chosen_ref), (tok_hbm, tok_ref), (up_hbm, up_ref))
    loads = [pltpu.make_async_copy(a, b, sem.at[i]) for i, (a, b) in enumerate(pairs)]
    for load in loads:
        load.start()
    loads[0].wait()
    col = lax.axis_index("expert")
    experts, cap = chosen_ref.shape
    count = tok_ref.shape[0]
    slots = experts * SLOT
    token = iota((count, cap), 0) + col * count
    lane = iota((count, experts), 1)
    mask = jnp.zeros((count, experts), F32)
    for e in range(experts):
        hit = jnp.sum((chosen_ref[e : e + 1, :] == token).astype(F32), axis=1, keepdims=True)
        mask = jnp.where(lane == e, hit, mask)
    mask = mask.astype(BF16)
    earlier = (iota((count, count), 0) > iota((count, count), 1)).astype(F32).astype(BF16)
    rank = mm(earlier, mask).astype(BF16)
    spread = (iota((experts, slots), 1) // SLOT == iota((experts, slots), 0)).astype(F32).astype(BF16)
    place = (iota((count, slots), 1) % SLOT).astype(F32)
    sender = jnp.logical_and(mm(mask, spread) > 0.5, mm(rank, spread) == place).astype(F32).astype(BF16)
    sender_ref[...] = sender
    loads[1].wait()
    loads[2].wait()
    blocks_ref[...] = mm(sender, jnp.concatenate([tok_ref[...], up_ref[...]], axis=1), FIRST).astype(BF16)
    own = chosen_ref[pl.ds(col, 1), :] // count
    block = iota((slots, cap), 0) // SLOT
    held = jnp.sum((own == block).astype(F32), axis=1, keepdims=True)
    before = jnp.sum((own < block).astype(F32), axis=1, keepdims=True)
    place = (iota((slots, 1), 0) % SLOT).astype(F32)
    row = jnp.where(place < held, before + place, -1.0)
    packer_ref[...] = (row == iota((slots, cap), 1).astype(F32)).astype(F32).astype(BF16)


def scale_up(rows):
    top = jnp.max(jnp.max(jnp.abs(rows), axis=1, keepdims=True), axis=0, keepdims=True)
    power = jnp.zeros_like(top)
    factor = jnp.full_like(top, 2.0**BASE)
    for step in STEPS:
        small = top <= 2.0 ** (2 - step)
        top = jnp.where(small, top * 2.0**step, top)
        factor = jnp.where(small, factor * 2.0**step, factor)
        power = jnp.where(small, power + step, power)
    return rows * factor, power


def pack_kernel(arrived_ref, packer_ref, out_ref):
    cap = packer_ref.shape[1]
    half = arrived_ref.shape[1] // 2
    rows = mm(packer_ref[...], arrived_ref[...], FIRST)
    for part in range(2):
        lanes = slice(part * half, (part + 1) * half)
        scaled, power = scale_up(rows[:, lanes])
        out_ref[:cap, lanes] = scaled.astype(BF16)
        out_ref[cap:, lanes] = jnp.broadcast_to(power, (out_ref.shape[0] - cap, half)).astype(BF16)


def expert_kernel(x_ref, gate_ref, up_ref, down_ref, router_ref, sib_ref, grads_ref, slope_ref, row_ref):
    col = lax.axis_index("expert")
    hidden = lax.axis_index("hidden")
    core = hidden % 2
    chips = x_ref.shape[0] // 2
    rows = x_ref.shape[1]
    width = gate_ref.shape[1]
    picks = iota(router_ref.shape, 0) == col
    router = jnp.sum(jnp.where(picks, router_ref[...].astype(F32), 0.0), axis=0, keepdims=True)
    row_ref[...] = router

    def at(j):
        return slice(2 * j * width, 2 * (j + 1) * width)

    pre = jnp.zeros((rows, 2 * width), F32)
    back = jnp.zeros((rows, width), F32)
    logit = jnp.zeros((rows, width), F32)
    for j in range(chips):
        x = jnp.concatenate([x_ref[2 * j, :, :width], x_ref[2 * j + 1, :, :width]], axis=1)
        u = jnp.concatenate([x_ref[2 * j, :, width:], x_ref[2 * j + 1, :, width:]], axis=1)
        pre += mm(x, jnp.concatenate([gate_ref[at(j), :], up_ref[at(j), :]], axis=1))
        back += mm(u, down_ref[:, at(j)], LAST)
        logged = x.astype(F32) * router[:, at(j)]
        logit += logged[:, :width] + logged[:, width:]
    logit = jnp.sum(logit, axis=1, keepdims=True)
    weight = 1.0 / (1.0 + jnp.exp(-logit))
    gate_pre, up_pre = pre[:, :width], pre[:, width:]
    sig = 1.0 / (1.0 + jnp.exp(-gate_pre))
    act = (gate_pre * sig * up_pre).astype(BF16)
    score = jnp.sum(back * act.astype(F32), axis=1, keepdims=True)
    scaled = weight * back
    d_up = (scaled * gate_pre * sig).astype(BF16)
    d_gate = (scaled * up_pre * sig * (1.0 + gate_pre * (1.0 - sig))).astype(BF16)
    grads = jnp.concatenate([d_gate, d_up], axis=1)
    slope = score * (weight * (1.0 - weight))

    grads_ref[...] = grads
    slope_ref[...] = jnp.broadcast_to(slope, slope_ref.shape)
    for apart in range(4):
        core_terms(apart, chips, 1 - core, grads, slope, gate_ref, up_ref, row_ref, sib_ref)


def core_terms(apart, chips, core, grads, slope, gate_ref, up_ref, row_ref, out_ref):
    chip = lax.axis_index("hidden") // 2
    width = gate_ref.shape[1]
    part = chips // 4

    def features(r):
        target = 4 * r + (chip + apart) % 4
        return pl.ds(pl.multiple_of((2 * target + core) * width, width), width)

    for first in range(0, part, 2):
        group = range(first, min(first + 2, part))
        side = [jnp.concatenate([gate_ref[features(r), :], up_ref[features(r), :]], axis=1) for r in group]
        terms = mm(grads, jnp.concatenate(side, axis=0), LAST)
        for i, r in enumerate(group):
            out = terms[:, i * width : (i + 1) * width] + slope * row_ref[:, features(r)]
            out_ref[apart * part + r] = out.astype(out_ref.dtype)


def terms_kernel(grads_ref, slope_ref, row_ref, gate_ref, up_ref, own_ref):
    core = lax.axis_index("hidden") % 2
    chips = gate_ref.shape[0] // (2 * gate_ref.shape[1])
    for apart in range(4):
        core_terms(apart, chips, core, grads_ref[...], slope_ref[:, :1], gate_ref, up_ref, row_ref, own_ref)


def body(tokens, upstream, router, w_gate, w_up, w_down, chosen):
    experts = lax.axis_size("expert")
    devices = lax.axis_size("hidden")
    chips = devices // 2
    count, width = tokens.shape
    cap = chosen.shape[1]
    slots = experts * SLOT

    blocks, sender, packer = call(
        route_kernel,
        [shape((slots, 2 * width), BF16), shape((count, slots), BF16), shape((slots, cap), BF16)],
        chosen, tokens, upstream,
        vmem=60,
        stream=True,
        scratch=[
            pltpu.VMEM(chosen.shape, jnp.int32),
            pltpu.VMEM(tokens.shape, BF16),
            pltpu.VMEM(upstream.shape, BF16),
            pltpu.SemaphoreType.DMA((3,)),
        ],
    )
    arrived = lax.all_to_all(blocks.reshape(experts, SLOT, 2 * width), "expert", 0, 0, tiled=True)
    (rows,) = call(pack_kernel, [shape((cap + 16, 2 * width), BF16)], arrived.reshape(slots, 2 * width), packer)
    full = lax.all_gather(rows.astype(jnp.float16), "hidden", axis=0)
    undo = jnp.exp2(-(full[:, cap : cap + 1, :].astype(F32) + BASE))
    picked = (full[:, :cap, :].astype(F32) * undo).astype(BF16)

    gate, up = w_gate[0], w_up[0]
    sibling, grads, slope, row = call(
        expert_kernel,
        [
            shape((chips, cap, width), BF16), shape((cap, 2 * width), BF16), shape((cap, width), F32),
            shape((1, devices * width), F32),
        ],
        picked, gate, up, w_down[0], router.T,
        flops=8 * cap * devices * width * width,
        vmem=24,
    )
    arrived = lax.ppermute(sibling, "hidden", [(i, i ^ 1) for i in range(devices)])
    (own,) = call(
        terms_kernel,
        [shape((chips, cap, width), F32)],
        grads, slope, row, gate, up,
        flops=8 * cap * devices * width * width,
        vmem=24,
    )

    def shift(v, hops):
        return lax.ppermute(v, "hidden", [(i, (i + 2 * hops) % devices) for i in range(devices)])

    part = chips // 4
    mid = cap // 2

    def both(group, lines):
        at = slice(group * part, (group + 1) * part)
        return own[at, lines] + arrived[at, lines].astype(F32)

    every = slice(0, cap)
    two_up = shift(both(2, slice(0, mid)).astype(BF16), 2)
    two_down = shift(both(2, slice(mid, cap)).astype(BF16), -2)
    one_up = shift(both(1, every).astype(BF16), 1)
    one_down = shift(both(3, every).astype(BF16), -1)
    two = jnp.concatenate([two_up, two_down], axis=1).astype(F32)
    near = (both(0, every) + one_up.astype(F32) + one_down.astype(F32) + two).astype(BF16)
    groups = [[c + 2 * q + 8 * r for r in range(part)] for q in range(4) for c in range(2)]
    parts = lax.all_to_all(near, "hidden", 0, 0, tiled=True, axis_index_groups=groups)
    slot_grad = jnp.sum(parts.astype(F32), axis=0).astype(BF16)
    outgoing = mm(packer, slot_grad).astype(BF16)
    arrived = lax.all_to_all(outgoing.reshape(experts, SLOT, width), "expert", 0, 0, tiled=True)
    return mm(sender, arrived.reshape(slots, width)).astype(BF16)


def solution(mesh):
    in_specs = (
        P("expert", "hidden"),
        P("expert", "hidden"),
        P(),
        P("expert", None, "hidden"),
        P("expert", None, "hidden"),
        P("expert", "hidden", None),
        P(),
    )
    out_specs = P("expert", "hidden")
    return jax.shard_map(body, mesh=mesh, in_specs=in_specs, out_specs=out_specs, check_vma=False)
```

```python
import jax
import jax.numpy as jnp
from jax import lax
from jax.experimental import pallas as pl
from jax.experimental.pallas import tpu as pltpu
from jax.sharding import PartitionSpec as P

F32 = jnp.float32
BF16 = jnp.bfloat16
SLOT = 16
LAST = (((1,), (1,)), ((), ()))
FIRST = (((0,), (0,)), ((), ()))
STEPS = (64, 16, 8, 4, 2, 1)
BASE = 13


def mm(a, b, dims=(((1,), (0,)), ((), ()))):
    return lax.dot_general(a, b, dims, preferred_element_type=F32)


def call(kernel, out, *args, flops=0, vmem=16):
    spec = pl.BlockSpec(memory_space=pltpu.VMEM)
    moved = sum(a.size * a.dtype.itemsize for a in args) + sum(o.size * o.dtype.itemsize for o in out)
    return pl.pallas_call(
        kernel,
        out_shape=list(out),
        in_specs=[spec] * len(args),
        out_specs=[spec] * len(out),
        compiler_params=pltpu.CompilerParams(vmem_limit_bytes=vmem * 1024 * 1024),
        cost_estimate=pl.CostEstimate(flops=flops, bytes_accessed=moved, transcendentals=0),
    )(*args)


def shape(dims, dtype):
    return jax.ShapeDtypeStruct(dims, dtype)


def iota(dims, axis):
    return lax.broadcasted_iota(jnp.int32, dims, axis)


def route_kernel(chosen_ref, both_ref, blocks_ref, sender_ref, packer_ref):
    col = lax.axis_index("expert")
    experts, cap = chosen_ref.shape
    count = both_ref.shape[0]
    slots = experts * SLOT
    token = iota((count, cap), 0) + col * count
    lane = iota((count, experts), 1)
    mask = jnp.zeros((count, experts), F32)
    for e in range(experts):
        hit = jnp.sum((chosen_ref[e : e + 1, :] == token).astype(F32), axis=1, keepdims=True)
        mask = jnp.where(lane == e, hit, mask)
    mask = mask.astype(BF16)
    earlier = (iota((count, count), 0) > iota((count, count), 1)).astype(F32).astype(BF16)
    rank = mm(earlier, mask).astype(BF16)
    spread = (iota((experts, slots), 1) // SLOT == iota((experts, slots), 0)).astype(F32).astype(BF16)
    place = (iota((count, slots), 1) % SLOT).astype(F32)
    sender = jnp.logical_and(mm(mask, spread) > 0.5, mm(rank, spread) == place).astype(F32).astype(BF16)
    sender_ref[...] = sender
    blocks_ref[...] = mm(sender, both_ref[...], FIRST).astype(BF16)
    own = chosen_ref[pl.ds(col, 1), :] // count
    block = iota((slots, cap), 0) // SLOT
    held = jnp.sum((own == block).astype(F32), axis=1, keepdims=True)
    before = jnp.sum((own < block).astype(F32), axis=1, keepdims=True)
    place = (iota((slots, 1), 0) % SLOT).astype(F32)
    row = jnp.where(place < held, before + place, -1.0)
    packer_ref[...] = (row == iota((slots, cap), 1).astype(F32)).astype(F32).astype(BF16)


def scale_up(rows):
    top = jnp.max(jnp.max(jnp.abs(rows), axis=1, keepdims=True), axis=0, keepdims=True)
    power = jnp.zeros_like(top)
    factor = jnp.full_like(top, 2.0**BASE)
    for step in STEPS:
        small = top <= 2.0 ** (2 - step)
        top = jnp.where(small, top * 2.0**step, top)
        factor = jnp.where(small, factor * 2.0**step, factor)
        power = jnp.where(small, power + step, power)
    return rows * factor, power


def pack_kernel(arrived_ref, packer_ref, out_ref):
    cap = packer_ref.shape[1]
    half = arrived_ref.shape[1] // 2
    rows = mm(packer_ref[...], arrived_ref[...], FIRST)
    for part in range(2):
        lanes = slice(part * half, (part + 1) * half)
        scaled, power = scale_up(rows[:, lanes])
        out_ref[:cap, lanes] = scaled.astype(BF16)
        out_ref[cap:, lanes] = jnp.broadcast_to(power, (out_ref.shape[0] - cap, half)).astype(BF16)


def expert_kernel(x_ref, gate_ref, up_ref, down_ref, router_ref, one_up_ref, one_down_ref, two_low_ref, two_high_ref, keep_ref, row_ref):
    hidden = lax.axis_index("hidden")
    core, chip = hidden % 2, hidden // 2
    chips = x_ref.shape[0] // 2
    rows = x_ref.shape[1]
    width = gate_ref.shape[2]
    part = chips // 4
    mid = rows // 2
    own = iota(router_ref.shape, 0) == lax.axis_index("expert")
    router = jnp.sum(jnp.where(own, router_ref[...].astype(F32), 0.0), axis=0, keepdims=True)
    row_ref[...] = router

    def wide(at):
        return jnp.concatenate([gate_ref[0, at, :], gate_ref[1, at, :], up_ref[0, at, :], up_ref[1, at, :]], axis=1)

    pre = jnp.zeros((rows, 4 * width), F32)
    back = jnp.zeros((rows, 2 * width), F32)
    logit = jnp.zeros((rows, width), F32)
    for j in range(chips):
        at = slice(2 * j * width, 2 * (j + 1) * width)
        x = jnp.concatenate([x_ref[2 * j, :, :width], x_ref[2 * j + 1, :, :width]], axis=1)
        u = jnp.concatenate([x_ref[2 * j, :, width:], x_ref[2 * j + 1, :, width:]], axis=1)
        pre += mm(x, wide(at))
        back += mm(u, jnp.concatenate([down_ref[0, :, at], down_ref[1, :, at]], axis=0), LAST)
        logged = x.astype(F32) * router[:, at]
        logit += logged[:, :width] + logged[:, width:]
    logit = jnp.sum(logit, axis=1, keepdims=True)
    weight = 1.0 / (1.0 + jnp.exp(-logit))
    gate_pre, up_pre = pre[:, : 2 * width], pre[:, 2 * width :]
    sig = 1.0 / (1.0 + jnp.exp(-gate_pre))
    act = (gate_pre * sig * up_pre).astype(BF16)
    score = jnp.sum(back * act.astype(F32), axis=1, keepdims=True)
    scaled = weight * back
    d_up = (scaled * gate_pre * sig).astype(BF16)
    d_gate = (scaled * up_pre * sig * (1.0 + gate_pre * (1.0 - sig))).astype(BF16)
    grads = jnp.concatenate([d_gate, d_up], axis=1)
    slope = score * (weight * (1.0 - weight))

    def features(apart, r):
        target = 4 * r + (chip + apart) % 4
        return pl.ds(pl.multiple_of((2 * target + core) * width, width), width)

    for apart in (1, 3, 2, 0):
        for first in range(0, part, 2):
            group = range(first, min(first + 2, part))
            terms = mm(grads, jnp.concatenate([wide(features(apart, r)) for r in group], axis=0), LAST)
            for i, r in enumerate(group):
                out = terms[:, i * width : (i + 1) * width] + slope * row_ref[:, features(apart, r)]
                if apart == 1:
                    one_up_ref[r] = out.astype(BF16)
                elif apart == 3:
                    one_down_ref[r] = out.astype(BF16)
                elif apart == 2:
                    two_low_ref[r] = out[:mid].astype(BF16)
                    two_high_ref[r] = out[mid:].astype(BF16)
                else:
                    keep_ref[r] = out


def body(tokens, upstream, router, w_gate, w_up, w_down, chosen):
    experts = lax.axis_size("expert")
    devices = lax.axis_size("hidden")
    chips = devices // 2
    count, width = tokens.shape
    cap = chosen.shape[1]
    slots = experts * SLOT

    blocks, sender, packer = call(
        route_kernel,
        [shape((slots, 2 * width), BF16), shape((count, slots), BF16), shape((slots, cap), BF16)],
        chosen, jnp.concatenate([tokens, upstream], axis=1),
    )
    cores = [[2 * z, 2 * z + 1] for z in range(chips)]
    gate, up, down = (lax.all_gather(w[0], "hidden", axis=0, axis_index_groups=cores) for w in (w_gate, w_up, w_down))
    arrived = lax.all_to_all(blocks.reshape(experts, SLOT, 2 * width), "expert", 0, 0, tiled=True)
    (rows,) = call(pack_kernel, [shape((cap + 16, 2 * width), BF16)], arrived.reshape(slots, 2 * width), packer)
    full = lax.all_gather(rows.astype(jnp.float16), "hidden", axis=0)
    full, gate, up, down = lax.optimization_barrier((full, gate, up, down))
    undo = jnp.exp2(-(full[:, cap : cap + 1, :].astype(F32) + BASE))
    picked = (full[:, :cap, :].astype(F32) * undo).astype(BF16)

    part = chips // 4
    mid = cap // 2
    full_rows, half_rows = (part, cap, width), (part, mid, width)
    one_up, one_down, two_low, two_high, keep, _ = call(
        expert_kernel,
        [
            shape(full_rows, BF16), shape(full_rows, BF16), shape(half_rows, BF16), shape(half_rows, BF16),
            shape(full_rows, F32), shape((1, devices * width), F32),
        ],
        picked, gate, up, down, router.T,
        flops=16 * cap * devices * width * width,
        vmem=24,
    )

    def shift(v, hops):
        return lax.ppermute(v, "hidden", [(i, (i + 2 * hops) % devices) for i in range(devices)])

    one = shift(one_up, 1).astype(F32) + shift(one_down, -1).astype(F32)
    two = jnp.concatenate([shift(two_low, 2), shift(two_high, -2)], axis=1).astype(F32)
    near = (keep + one + two).astype(BF16)
    groups = [[c + 2 * q + 8 * r for r in range(part)] for q in range(4) for c in range(2)]
    parts = lax.all_to_all(near, "hidden", 0, 0, tiled=True, axis_index_groups=groups)
    slot_grad = jnp.sum(parts.astype(F32), axis=0).astype(BF16)
    outgoing = mm(packer, slot_grad).astype(BF16)
    arrived = lax.all_to_all(outgoing.reshape(experts, SLOT, width), "expert", 0, 0, tiled=True)
    return mm(sender, arrived.reshape(slots, width)).astype(BF16)


def solution(mesh):
    in_specs = (
        P("expert", "hidden"),
        P("expert", "hidden"),
        P(),
        P("expert", None, "hidden"),
        P("expert", None, "hidden"),
        P("expert", "hidden", None),
        P(),
    )
    out_specs = P("expert", "hidden")
    return jax.shard_map(body, mesh=mesh, in_specs=in_specs, out_specs=out_specs, check_vma=False)
```

```python
import jax
import jax.numpy as jnp
from jax import lax
from jax.experimental import pallas as pl
from jax.experimental.pallas import tpu as pltpu
from jax.sharding import PartitionSpec as P

F32 = jnp.float32
BF16 = jnp.bfloat16
SLOT = 16
LAST = (((1,), (1,)), ((), ()))
FIRST = (((0,), (0,)), ((), ()))
STEPS = (64, 16, 8, 4, 2, 1)
BASE = 13


def mm(a, b, dims=(((1,), (0,)), ((), ()))):
    return lax.dot_general(a, b, dims, preferred_element_type=F32)


def call(kernel, out, *args, flops=0, vmem=16, stream=False, scratch=()):
    spec = pl.BlockSpec(memory_space=pltpu.VMEM)
    moved = sum(a.size * a.dtype.itemsize for a in args) + sum(o.size * o.dtype.itemsize for o in out)
    return pl.pallas_call(
        kernel,
        out_shape=list(out),
        in_specs=[pl.BlockSpec(memory_space=pltpu.HBM) if stream else spec] * len(args),
        out_specs=[spec] * len(out),
        scratch_shapes=list(scratch),
        compiler_params=pltpu.CompilerParams(vmem_limit_bytes=vmem * 1024 * 1024),
        cost_estimate=pl.CostEstimate(flops=flops, bytes_accessed=moved, transcendentals=0),
    )(*args)


def shape(dims, dtype):
    return jax.ShapeDtypeStruct(dims, dtype)


def iota(dims, axis):
    return lax.broadcasted_iota(jnp.int32, dims, axis)


def route_kernel(chosen_hbm, tok_hbm, up_hbm, blocks_ref, sender_ref, packer_ref, chosen_ref, tok_ref, up_ref, sem):
    pairs = ((chosen_hbm, chosen_ref), (tok_hbm, tok_ref), (up_hbm, up_ref))
    loads = [pltpu.make_async_copy(a, b, sem.at[i]) for i, (a, b) in enumerate(pairs)]
    for load in loads:
        load.start()
    loads[0].wait()
    col = lax.axis_index("expert")
    experts, cap = chosen_ref.shape
    count = tok_ref.shape[0]
    slots = experts * SLOT
    token = iota((count, cap), 0) + col * count
    lane = iota((count, experts), 1)
    mask = jnp.zeros((count, experts), F32)
    for e in range(experts):
        hit = jnp.sum((chosen_ref[e : e + 1, :] == token).astype(F32), axis=1, keepdims=True)
        mask = jnp.where(lane == e, hit, mask)
    mask = mask.astype(BF16)
    earlier = (iota((count, count), 0) > iota((count, count), 1)).astype(F32).astype(BF16)
    rank = mm(earlier, mask).astype(BF16)
    spread = (iota((experts, slots), 1) // SLOT == iota((experts, slots), 0)).astype(F32).astype(BF16)
    place = (iota((count, slots), 1) % SLOT).astype(F32)
    sender = jnp.logical_and(mm(mask, spread) > 0.5, mm(rank, spread) == place).astype(F32).astype(BF16)
    sender_ref[...] = sender
    loads[1].wait()
    loads[2].wait()
    blocks_ref[...] = mm(sender, jnp.concatenate([tok_ref[...], up_ref[...]], axis=1), FIRST).astype(BF16)
    own = chosen_ref[pl.ds(col, 1), :] // count
    block = iota((slots, cap), 0) // SLOT
    held = jnp.sum((own == block).astype(F32), axis=1, keepdims=True)
    before = jnp.sum((own < block).astype(F32), axis=1, keepdims=True)
    place = (iota((slots, 1), 0) % SLOT).astype(F32)
    row = jnp.where(place < held, before + place, -1.0)
    packer_ref[...] = (row == iota((slots, cap), 1).astype(F32)).astype(F32).astype(BF16)


def scale_up(rows):
    top = jnp.max(jnp.max(jnp.abs(rows), axis=1, keepdims=True), axis=0, keepdims=True)
    power = jnp.zeros_like(top)
    factor = jnp.full_like(top, 2.0**BASE)
    for step in STEPS:
        small = top <= 2.0 ** (2 - step)
        top = jnp.where(small, top * 2.0**step, top)
        factor = jnp.where(small, factor * 2.0**step, factor)
        power = jnp.where(small, power + step, power)
    return rows * factor, power


def pack_kernel(arrived_ref, packer_ref, out_ref):
    cap = packer_ref.shape[1]
    half = arrived_ref.shape[1] // 2
    rows = mm(packer_ref[...], arrived_ref[...], FIRST)
    for part in range(2):
        lanes = slice(part * half, (part + 1) * half)
        scaled, power = scale_up(rows[:, lanes])
        out_ref[:cap, lanes] = scaled.astype(BF16)
        out_ref[cap:, lanes] = jnp.broadcast_to(power, (out_ref.shape[0] - cap, half)).astype(BF16)


def expert_kernel(x_ref, gate_ref, up_ref, down_ref, router_ref, sib_ref, grads_ref, slope_ref, row_ref):
    col = lax.axis_index("expert")
    hidden = lax.axis_index("hidden")
    core = hidden % 2
    chips = x_ref.shape[0] // 2
    rows = x_ref.shape[1]
    width = gate_ref.shape[1]
    picks = iota(router_ref.shape, 0) == col
    router = jnp.sum(jnp.where(picks, router_ref[...].astype(F32), 0.0), axis=0, keepdims=True)
    row_ref[...] = router

    def at(j):
        return slice(2 * j * width, 2 * (j + 1) * width)

    pre = jnp.zeros((rows, 2 * width), F32)
    back = jnp.zeros((rows, width), F32)
    logit = jnp.zeros((rows, width), F32)
    for j in range(chips):
        x = jnp.concatenate([x_ref[2 * j, :, :width], x_ref[2 * j + 1, :, :width]], axis=1)
        u = jnp.concatenate([x_ref[2 * j, :, width:], x_ref[2 * j + 1, :, width:]], axis=1)
        pre += mm(x, jnp.concatenate([gate_ref[at(j), :], up_ref[at(j), :]], axis=1))
        back += mm(u, down_ref[:, at(j)], LAST)
        logged = x.astype(F32) * router[:, at(j)]
        logit += logged[:, :width] + logged[:, width:]
    logit = jnp.sum(logit, axis=1, keepdims=True)
    weight = 1.0 / (1.0 + jnp.exp(-logit))
    gate_pre, up_pre = pre[:, :width], pre[:, width:]
    sig = 1.0 / (1.0 + jnp.exp(-gate_pre))
    act = (gate_pre * sig * up_pre).astype(BF16)
    score = jnp.sum(back * act.astype(F32), axis=1, keepdims=True)
    scaled = weight * back
    d_up = (scaled * gate_pre * sig).astype(BF16)
    d_gate = (scaled * up_pre * sig * (1.0 + gate_pre * (1.0 - sig))).astype(BF16)
    grads = jnp.concatenate([d_gate, d_up], axis=1)
    slope = score * (weight * (1.0 - weight))

    grads_ref[...] = grads
    slope_ref[...] = jnp.broadcast_to(slope, slope_ref.shape)
    for apart in range(4):
        core_terms(apart, chips, 1 - core, grads, slope, gate_ref, up_ref, row_ref, sib_ref)


def core_terms(apart, chips, core, grads, slope, gate_ref, up_ref, row_ref, out_ref):
    chip = lax.axis_index("hidden") // 2
    width = gate_ref.shape[1]
    part = chips // 4

    def features(r):
        target = 4 * r + (chip + apart) % 4
        return pl.ds(pl.multiple_of((2 * target + core) * width, width), width)

    for first in range(0, part, 2):
        group = range(first, min(first + 2, part))
        side = [jnp.concatenate([gate_ref[features(r), :], up_ref[features(r), :]], axis=1) for r in group]
        terms = mm(grads, jnp.concatenate(side, axis=0), LAST)
        for i, r in enumerate(group):
            out = terms[:, i * width : (i + 1) * width] + slope * row_ref[:, features(r)]
            out_ref[apart * part + r] = out.astype(out_ref.dtype)


def terms_kernel(grads_ref, slope_ref, row_ref, gate_ref, up_ref, own_ref):
    core = lax.axis_index("hidden") % 2
    chips = gate_ref.shape[0] // (2 * gate_ref.shape[1])
    for apart in range(4):
        core_terms(apart, chips, core, grads_ref[...], slope_ref[:, :1], gate_ref, up_ref, row_ref, own_ref)


def body(tokens, upstream, router, w_gate, w_up, w_down, chosen):
    experts = lax.axis_size("expert")
    devices = lax.axis_size("hidden")
    chips = devices // 2
    count, width = tokens.shape
    cap = chosen.shape[1]
    slots = experts * SLOT

    blocks, sender, packer = call(
        route_kernel,
        [shape((slots, 2 * width), BF16), shape((count, slots), BF16), shape((slots, cap), BF16)],
        chosen, tokens, upstream,
        stream=True,
        scratch=[
            pltpu.VMEM(chosen.shape, jnp.int32),
            pltpu.VMEM(tokens.shape, BF16),
            pltpu.VMEM(upstream.shape, BF16),
            pltpu.SemaphoreType.DMA((3,)),
        ],
    )
    arrived = lax.all_to_all(blocks.reshape(experts, SLOT, 2 * width), "expert", 0, 0, tiled=True)
    (rows,) = call(pack_kernel, [shape((cap + 16, 2 * width), BF16)], arrived.reshape(slots, 2 * width), packer)
    full = lax.all_gather(rows.astype(jnp.float16), "hidden", axis=0)
    undo = jnp.exp2(-(full[:, cap : cap + 1, :].astype(F32) + BASE))
    picked = (full[:, :cap, :].astype(F32) * undo).astype(BF16)

    gate, up = w_gate[0], w_up[0]
    sibling, grads, slope, row = call(
        expert_kernel,
        [
            shape((chips, cap, width), BF16), shape((cap, 2 * width), BF16), shape((cap, width), F32),
            shape((1, devices * width), F32),
        ],
        picked, gate, up, w_down[0], router.T,
        flops=8 * cap * devices * width * width,
        vmem=24,
    )
    arrived = lax.ppermute(sibling, "hidden", [(i, i ^ 1) for i in range(devices)])
    (own,) = call(
        terms_kernel,
        [shape((chips, cap, width), F32)],
        grads, slope, row, gate, up,
        flops=8 * cap * devices * width * width,
        vmem=24,
    )

    part = chips // 4

    def both(apart):
        at = slice(apart * part, (apart + 1) * part)
        return own[at] + arrived[at].astype(F32)

    def shift(apart, hops):
        to = [(i, (i + 2 * hops[i % 2]) % devices) for i in range(devices)]
        return lax.ppermute(both(apart).astype(BF16), "hidden", to).astype(F32)

    near = (both(0) + shift(1, (1, 1)) + shift(3, (-1, -1)) + shift(2, (2, -2))).astype(BF16)
    groups = [[c + 2 * q + 8 * r for r in range(part)] for q in range(4) for c in range(2)]
    parts = lax.all_to_all(near, "hidden", 0, 0, tiled=True, axis_index_groups=groups)
    slot_grad = jnp.sum(parts.astype(F32), axis=0).astype(BF16)
    outgoing = mm(packer, slot_grad).astype(BF16)
    arrived = lax.all_to_all(outgoing.reshape(experts, SLOT, width), "expert", 0, 0, tiled=True)
    return mm(sender, arrived.reshape(slots, width)).astype(BF16)


def solution(mesh):
    in_specs = (
        P("expert", "hidden"),
        P("expert", "hidden"),
        P(),
        P("expert", None, "hidden"),
        P("expert", None, "hidden"),
        P("expert", "hidden", None),
        P(),
    )
    out_specs = P("expert", "hidden")
    return jax.shard_map(body, mesh=mesh, in_specs=in_specs, out_specs=out_specs, check_vma=False)
```

```python
import jax
import jax.numpy as jnp
from jax import lax
from jax.experimental import pallas as pl
from jax.experimental.pallas import tpu as pltpu
from jax.sharding import PartitionSpec as P

F32 = jnp.float32
BF16 = jnp.bfloat16
SLOT = 16
LAST = (((1,), (1,)), ((), ()))
FIRST = (((0,), (0,)), ((), ()))
STEPS = (64, 16, 8, 4, 2, 1)
BASE = 13


def mm(a, b, dims=(((1,), (0,)), ((), ()))):
    return lax.dot_general(a, b, dims, preferred_element_type=F32)


def call(kernel, out, *args, flops=0, vmem=16, stream=False, scratch=()):
    spec = pl.BlockSpec(memory_space=pltpu.VMEM)
    moved = sum(a.size * a.dtype.itemsize for a in args) + sum(o.size * o.dtype.itemsize for o in out)
    return pl.pallas_call(
        kernel,
        out_shape=list(out),
        in_specs=[pl.BlockSpec(memory_space=pltpu.HBM) if stream else spec] * len(args),
        out_specs=[spec] * len(out),
        scratch_shapes=list(scratch),
        compiler_params=pltpu.CompilerParams(vmem_limit_bytes=vmem * 1024 * 1024),
        cost_estimate=pl.CostEstimate(flops=flops, bytes_accessed=moved, transcendentals=0),
    )(*args)


def shape(dims, dtype):
    return jax.ShapeDtypeStruct(dims, dtype)


def iota(dims, axis):
    return lax.broadcasted_iota(jnp.int32, dims, axis)


def route_kernel(chosen_hbm, tok_hbm, up_hbm, blocks_ref, sender_ref, packer_ref, chosen_ref, tok_ref, up_ref, sem):
    pairs = ((chosen_hbm, chosen_ref), (tok_hbm, tok_ref), (up_hbm, up_ref))
    loads = [pltpu.make_async_copy(a, b, sem.at[i]) for i, (a, b) in enumerate(pairs)]
    for load in loads:
        load.start()
    loads[0].wait()
    col = lax.axis_index("expert")
    experts, cap = chosen_ref.shape
    count = tok_ref.shape[0]
    slots = experts * SLOT
    token = iota((count, cap), 0) + col * count
    lane = iota((count, experts), 1)
    mask = jnp.zeros((count, experts), F32)
    for e in range(experts):
        hit = jnp.sum((chosen_ref[e : e + 1, :] == token).astype(F32), axis=1, keepdims=True)
        mask = jnp.where(lane == e, hit, mask)
    mask = mask.astype(BF16)
    earlier = (iota((count, count), 0) > iota((count, count), 1)).astype(F32).astype(BF16)
    rank = mm(earlier, mask).astype(BF16)
    spread = (iota((experts, slots), 1) // SLOT == iota((experts, slots), 0)).astype(F32).astype(BF16)
    place = (iota((count, slots), 1) % SLOT).astype(F32)
    sender = jnp.logical_and(mm(mask, spread) > 0.5, mm(rank, spread) == place).astype(F32).astype(BF16)
    sender_ref[...] = sender
    loads[1].wait()
    loads[2].wait()
    blocks_ref[...] = mm(sender, jnp.concatenate([tok_ref[...], up_ref[...]], axis=1), FIRST).astype(BF16)
    own = chosen_ref[pl.ds(col, 1), :] // count
    block = iota((slots, cap), 0) // SLOT
    held = jnp.sum((own == block).astype(F32), axis=1, keepdims=True)
    before = jnp.sum((own < block).astype(F32), axis=1, keepdims=True)
    place = (iota((slots, 1), 0) % SLOT).astype(F32)
    row = jnp.where(place < held, before + place, -1.0)
    packer_ref[...] = (row == iota((slots, cap), 1).astype(F32)).astype(F32).astype(BF16)


def scale_up(rows):
    top = jnp.max(jnp.max(jnp.abs(rows), axis=1, keepdims=True), axis=0, keepdims=True)
    power = jnp.zeros_like(top)
    factor = jnp.full_like(top, 2.0**BASE)
    for step in STEPS:
        small = top <= 2.0 ** (2 - step)
        top = jnp.where(small, top * 2.0**step, top)
        factor = jnp.where(small, factor * 2.0**step, factor)
        power = jnp.where(small, power + step, power)
    return rows * factor, power


def pack_kernel(arrived_ref, packer_ref, out_ref):
    cap = packer_ref.shape[1]
    half = arrived_ref.shape[1] // 2
    rows = mm(packer_ref[...], arrived_ref[...], FIRST)
    for part in range(2):
        lanes = slice(part * half, (part + 1) * half)
        scaled, power = scale_up(rows[:, lanes])
        out_ref[:cap, lanes] = scaled.astype(BF16)
        out_ref[cap:, lanes] = jnp.broadcast_to(power, (out_ref.shape[0] - cap, half)).astype(BF16)


def expert_kernel(x_ref, gate_ref, up_ref, down_ref, router_ref, sib_ref, grads_ref, slope_ref, row_ref):
    col = lax.axis_index("expert")
    hidden = lax.axis_index("hidden")
    core = hidden % 2
    chips = x_ref.shape[0] // 2
    rows = x_ref.shape[1]
    width = gate_ref.shape[1]
    picks = iota(router_ref.shape, 0) == col
    router = jnp.sum(jnp.where(picks, router_ref[...].astype(F32), 0.0), axis=0, keepdims=True)
    row_ref[...] = router

    def at(j):
        return slice(2 * j * width, 2 * (j + 1) * width)

    pre = jnp.zeros((rows, 2 * width), F32)
    back = jnp.zeros((rows, width), F32)
    logit = jnp.zeros((rows, width), F32)
    for j in range(chips):
        x = jnp.concatenate([x_ref[2 * j, :, :width], x_ref[2 * j + 1, :, :width]], axis=1)
        u = jnp.concatenate([x_ref[2 * j, :, width:], x_ref[2 * j + 1, :, width:]], axis=1)
        pre += mm(x, jnp.concatenate([gate_ref[at(j), :], up_ref[at(j), :]], axis=1))
        back += mm(u, down_ref[:, at(j)], LAST)
        logged = x.astype(F32) * router[:, at(j)]
        logit += logged[:, :width] + logged[:, width:]
    logit = jnp.sum(logit, axis=1, keepdims=True)
    weight = 1.0 / (1.0 + jnp.exp(-logit))
    gate_pre, up_pre = pre[:, :width], pre[:, width:]
    sig = 1.0 / (1.0 + jnp.exp(-gate_pre))
    act = (gate_pre * sig * up_pre).astype(BF16)
    score = jnp.sum(back * act.astype(F32), axis=1, keepdims=True)
    scaled = weight * back
    d_up = (scaled * gate_pre * sig).astype(BF16)
    d_gate = (scaled * up_pre * sig * (1.0 + gate_pre * (1.0 - sig))).astype(BF16)
    grads = jnp.concatenate([d_gate, d_up], axis=1)
    slope = score * (weight * (1.0 - weight))

    grads_ref[...] = grads
    slope_ref[...] = jnp.broadcast_to(slope, slope_ref.shape)
    core_terms(chips, 1 - core, grads, slope, gate_ref, up_ref, row_ref, sib_ref)


def core_terms(chips, core, grads, slope, gate_ref, up_ref, row_ref, out_ref):
    chip = lax.axis_index("hidden") // 2
    width = gate_ref.shape[1]
    part = chips // 4
    along = 1 + 2 * core
    for group, apart in enumerate((0, 4 - along, 2, along)):

        def features(r):
            target = 4 * r + (chip + apart) % 4
            return pl.ds(pl.multiple_of((2 * target + core) * width, width), width)

        for first in range(0, part, 2):
            some = range(first, min(first + 2, part))
            side = [jnp.concatenate([gate_ref[features(r), :], up_ref[features(r), :]], axis=1) for r in some]
            terms = mm(grads, jnp.concatenate(side, axis=0), LAST)
            for i, r in enumerate(some):
                out = terms[:, i * width : (i + 1) * width] + slope * row_ref[:, features(r)]
                out_ref[group * part + r] = out.astype(out_ref.dtype)


def terms_kernel(grads_ref, slope_ref, row_ref, gate_ref, up_ref, own_ref):
    core = lax.axis_index("hidden") % 2
    chips = gate_ref.shape[0] // (2 * gate_ref.shape[1])
    core_terms(chips, core, grads_ref[...], slope_ref[:, :1], gate_ref, up_ref, row_ref, own_ref)


def body(tokens, upstream, router, w_gate, w_up, w_down, chosen):
    experts = lax.axis_size("expert")
    devices = lax.axis_size("hidden")
    chips = devices // 2
    count, width = tokens.shape
    cap = chosen.shape[1]
    slots = experts * SLOT

    blocks, sender, packer = call(
        route_kernel,
        [shape((slots, 2 * width), BF16), shape((count, slots), BF16), shape((slots, cap), BF16)],
        chosen, tokens, upstream,
        stream=True,
        scratch=[
            pltpu.VMEM(chosen.shape, jnp.int32),
            pltpu.VMEM(tokens.shape, BF16),
            pltpu.VMEM(upstream.shape, BF16),
            pltpu.SemaphoreType.DMA((3,)),
        ],
    )
    arrived = lax.all_to_all(blocks.reshape(experts, SLOT, 2 * width), "expert", 0, 0, tiled=True)
    (rows,) = call(pack_kernel, [shape((cap + 16, 2 * width), BF16)], arrived.reshape(slots, 2 * width), packer)
    full = lax.all_gather(rows.astype(jnp.float16), "hidden", axis=0)
    undo = jnp.exp2(-(full[:, cap : cap + 1, :].astype(F32) + BASE))
    picked = (full[:, :cap, :].astype(F32) * undo).astype(BF16)

    gate, up = w_gate[0], w_up[0]
    sibling, grads, slope, row = call(
        expert_kernel,
        [
            shape((chips, cap, width), BF16), shape((cap, 2 * width), BF16), shape((cap, width), F32),
            shape((1, devices * width), F32),
        ],
        picked, gate, up, w_down[0], router.T,
        flops=8 * cap * devices * width * width,
        vmem=24,
    )
    arrived = lax.ppermute(sibling, "hidden", [(i, i ^ 1) for i in range(devices)])
    (own,) = call(
        terms_kernel,
        [shape((chips, cap, width), F32)],
        grads, slope, row, gate, up,
        flops=8 * cap * devices * width * width,
        vmem=24,
    )

    part = chips // 4

    def both(group):
        at = slice(group * part, (group + 1) * part)
        return own[at] + arrived[at].astype(F32)

    def shift(v, hops):
        to = [(i, (i + 2 * hops * (1 - 2 * (i % 2))) % devices) for i in range(devices)]
        return lax.ppermute(v.astype(BF16), "hidden", to).astype(F32)

    passed = shift(both(2), 1)
    near = (both(0) + shift(both(1), -1) + shift(both(3) + passed, 1)).astype(BF16)
    groups = [[c + 2 * q + 8 * r for r in range(part)] for q in range(4) for c in range(2)]
    parts = lax.all_to_all(near, "hidden", 0, 0, tiled=True, axis_index_groups=groups)
    slot_grad = jnp.sum(parts.astype(F32), axis=0).astype(BF16)
    outgoing = mm(packer, slot_grad).astype(BF16)
    arrived = lax.all_to_all(outgoing.reshape(experts, SLOT, width), "expert", 0, 0, tiled=True)
    return mm(sender, arrived.reshape(slots, width)).astype(BF16)


def solution(mesh):
    in_specs = (
        P("expert", "hidden"),
        P("expert", "hidden"),
        P(),
        P("expert", None, "hidden"),
        P("expert", None, "hidden"),
        P("expert", "hidden", None),
        P(),
    )
    out_specs = P("expert", "hidden")
    return jax.shard_map(body, mesh=mesh, in_specs=in_specs, out_specs=out_specs, check_vma=False)
```

```python
import jax
import jax.numpy as jnp
from jax import lax
from jax.experimental import pallas as pl
from jax.experimental.pallas import tpu as pltpu
from jax.sharding import PartitionSpec as P

F32 = jnp.float32
BF16 = jnp.bfloat16
SLOT = 16
LAST = (((1,), (1,)), ((), ()))
FIRST = (((0,), (0,)), ((), ()))
STEPS = (64, 16, 8, 4, 2, 1)
BASE = 13


def mm(a, b, dims=(((1,), (0,)), ((), ()))):
    return lax.dot_general(a, b, dims, preferred_element_type=F32)


def call(kernel, out, *args, flops=0, vmem=16, stream=False, scratch=()):
    spec = pl.BlockSpec(memory_space=pltpu.VMEM)
    moved = sum(a.size * a.dtype.itemsize for a in args) + sum(o.size * o.dtype.itemsize for o in out)
    return pl.pallas_call(
        kernel,
        out_shape=list(out),
        in_specs=[pl.BlockSpec(memory_space=pltpu.HBM) if stream else spec] * len(args),
        out_specs=[spec] * len(out),
        scratch_shapes=list(scratch),
        compiler_params=pltpu.CompilerParams(vmem_limit_bytes=vmem * 1024 * 1024),
        cost_estimate=pl.CostEstimate(flops=flops, bytes_accessed=moved, transcendentals=0),
    )(*args)


def shape(dims, dtype):
    return jax.ShapeDtypeStruct(dims, dtype)


def iota(dims, axis):
    return lax.broadcasted_iota(jnp.int32, dims, axis)


def route_kernel(chosen_hbm, tok_hbm, up_hbm, blocks_ref, sender_ref, packer_ref, chosen_ref, tok_ref, up_ref, sem):
    pairs = ((chosen_hbm, chosen_ref), (tok_hbm, tok_ref), (up_hbm, up_ref))
    loads = [pltpu.make_async_copy(a, b, sem.at[i]) for i, (a, b) in enumerate(pairs)]
    for load in loads:
        load.start()
    loads[0].wait()
    col = lax.axis_index("expert")
    experts, cap = chosen_ref.shape
    count = tok_ref.shape[0]
    slots = experts * SLOT
    token = iota((count, cap), 0) + col * count
    lane = iota((count, experts), 1)
    mask = jnp.zeros((count, experts), F32)
    for e in range(experts):
        hit = jnp.sum((chosen_ref[e : e + 1, :] == token).astype(F32), axis=1, keepdims=True)
        mask = jnp.where(lane == e, hit, mask)
    mask = mask.astype(BF16)
    earlier = (iota((count, count), 0) > iota((count, count), 1)).astype(F32).astype(BF16)
    rank = mm(earlier, mask).astype(BF16)
    spread = (iota((experts, slots), 1) // SLOT == iota((experts, slots), 0)).astype(F32).astype(BF16)
    place = (iota((count, slots), 1) % SLOT).astype(F32)
    sender = jnp.logical_and(mm(mask, spread) > 0.5, mm(rank, spread) == place).astype(F32).astype(BF16)
    sender_ref[...] = sender
    loads[1].wait()
    loads[2].wait()
    blocks_ref[...] = mm(sender, jnp.concatenate([tok_ref[...], up_ref[...]], axis=1), FIRST).astype(BF16)
    own = chosen_ref[pl.ds(col, 1), :] // count
    block = iota((slots, cap), 0) // SLOT
    held = jnp.sum((own == block).astype(F32), axis=1, keepdims=True)
    before = jnp.sum((own < block).astype(F32), axis=1, keepdims=True)
    place = (iota((slots, 1), 0) % SLOT).astype(F32)
    row = jnp.where(place < held, before + place, -1.0)
    packer_ref[...] = (row == iota((slots, cap), 1).astype(F32)).astype(F32).astype(BF16)


def scale_up(rows):
    top = jnp.max(jnp.max(jnp.abs(rows), axis=1, keepdims=True), axis=0, keepdims=True)
    power = jnp.zeros_like(top)
    factor = jnp.full_like(top, 2.0**BASE)
    for step in STEPS:
        small = top <= 2.0 ** (2 - step)
        top = jnp.where(small, top * 2.0**step, top)
        factor = jnp.where(small, factor * 2.0**step, factor)
        power = jnp.where(small, power + step, power)
    return rows * factor, power


def pack_kernel(arrived_ref, packer_ref, out_ref):
    cap = packer_ref.shape[1]
    half = arrived_ref.shape[1] // 2
    rows = mm(packer_ref[...], arrived_ref[...], FIRST)
    for part in range(2):
        lanes = slice(part * half, (part + 1) * half)
        scaled, power = scale_up(rows[:, lanes])
        out_ref[:cap, lanes] = scaled.astype(BF16)
        out_ref[cap:, lanes] = jnp.broadcast_to(power, (out_ref.shape[0] - cap, half)).astype(BF16)


def expert_kernel(x_ref, gate_ref, up_ref, down_ref, router_ref, sib_ref, grads_ref, slope_ref, row_ref):
    col = lax.axis_index("expert")
    hidden = lax.axis_index("hidden")
    core = hidden % 2
    chips = x_ref.shape[0] // 2
    rows = x_ref.shape[1]
    width = gate_ref.shape[1]
    picks = iota(router_ref.shape, 0) == col
    router = jnp.sum(jnp.where(picks, router_ref[...].astype(F32), 0.0), axis=0, keepdims=True)
    row_ref[...] = router

    def at(j):
        return slice(2 * j * width, 2 * (j + 1) * width)

    pre = jnp.zeros((rows, 2 * width), F32)
    back = jnp.zeros((rows, width), F32)
    logit = jnp.zeros((rows, width), F32)
    for j in range(chips):
        x = jnp.concatenate([x_ref[2 * j, :, :width], x_ref[2 * j + 1, :, :width]], axis=1)
        u = jnp.concatenate([x_ref[2 * j, :, width:], x_ref[2 * j + 1, :, width:]], axis=1)
        pre += mm(x, jnp.concatenate([gate_ref[at(j), :], up_ref[at(j), :]], axis=1))
        back += mm(u, down_ref[:, at(j)], LAST)
        logged = x.astype(F32) * router[:, at(j)]
        logit += logged[:, :width] + logged[:, width:]
    logit = jnp.sum(logit, axis=1, keepdims=True)
    weight = 1.0 / (1.0 + jnp.exp(-logit))
    gate_pre, up_pre = pre[:, :width], pre[:, width:]
    sig = 1.0 / (1.0 + jnp.exp(-gate_pre))
    act = (gate_pre * sig * up_pre).astype(BF16)
    score = jnp.sum(back * act.astype(F32), axis=1, keepdims=True)
    scaled = weight * back
    d_up = (scaled * gate_pre * sig).astype(BF16)
    d_gate = (scaled * up_pre * sig * (1.0 + gate_pre * (1.0 - sig))).astype(BF16)
    grads = jnp.concatenate([d_gate, d_up], axis=1)
    slope = score * (weight * (1.0 - weight))

    grads_ref[...] = grads
    slope_ref[...] = jnp.broadcast_to(slope, slope_ref.shape)
    core_terms(chips, 1 - core, grads, slope, gate_ref, up_ref, row_ref, sib_ref)


def core_terms(chips, core, grads, slope, gate_ref, up_ref, row_ref, out_ref):
    chip = lax.axis_index("hidden") // 2
    width = gate_ref.shape[1]
    part = chips // 4
    along = 1 + 2 * core
    for group, apart in enumerate((0, 4 - along, 2, along)):

        def features(r):
            target = 4 * r + (chip + apart) % 4
            return pl.ds(pl.multiple_of((2 * target + core) * width, width), width)

        for first in range(0, part, 2):
            some = range(first, min(first + 2, part))
            side = [jnp.concatenate([gate_ref[features(r), :], up_ref[features(r), :]], axis=1) for r in some]
            terms = mm(grads, jnp.concatenate(side, axis=0), LAST)
            for i, r in enumerate(some):
                out = terms[:, i * width : (i + 1) * width] + slope * row_ref[:, features(r)]
                out_ref[group * part + r] = out.astype(out_ref.dtype)


def terms_kernel(grads_ref, slope_ref, row_ref, gate_ref, up_ref, own_ref):
    core = lax.axis_index("hidden") % 2
    chips = gate_ref.shape[0] // (2 * gate_ref.shape[1])
    core_terms(chips, core, grads_ref[...], slope_ref[:, :1], gate_ref, up_ref, row_ref, own_ref)


def body(tokens, upstream, router, w_gate, w_up, w_down, chosen):
    experts = lax.axis_size("expert")
    devices = lax.axis_size("hidden")
    chips = devices // 2
    count, width = tokens.shape
    cap = chosen.shape[1]
    slots = experts * SLOT

    blocks, sender, packer = call(
        route_kernel,
        [shape((slots, 2 * width), BF16), shape((count, slots), BF16), shape((slots, cap), BF16)],
        chosen, tokens, upstream,
        stream=True,
        scratch=[
            pltpu.VMEM(chosen.shape, jnp.int32),
            pltpu.VMEM(tokens.shape, BF16),
            pltpu.VMEM(upstream.shape, BF16),
            pltpu.SemaphoreType.DMA((3,)),
        ],
    )
    arrived = lax.all_to_all(blocks.reshape(experts, SLOT, 2 * width), "expert", 0, 0, tiled=True)
    (rows,) = call(pack_kernel, [shape((cap + 16, 2 * width), BF16)], arrived.reshape(slots, 2 * width), packer)
    full = lax.all_gather(rows.astype(jnp.float16), "hidden", axis=0)
    undo = jnp.exp2(-(full[:, cap : cap + 1, :].astype(F32) + BASE))
    picked = (full[:, :cap, :].astype(F32) * undo).astype(BF16)

    gate, up = w_gate[0], w_up[0]
    sibling, grads, slope, row = call(
        expert_kernel,
        [
            shape((chips, cap, width), BF16), shape((cap, 2 * width), BF16), shape((cap, width), F32),
            shape((1, devices * width), F32),
        ],
        picked, gate, up, w_down[0], router.T,
        flops=8 * cap * devices * width * width,
        vmem=24,
    )
    arrived = lax.ppermute(sibling, "hidden", [(i, i ^ 1) for i in range(devices)])
    (own,) = call(
        terms_kernel,
        [shape((chips, cap, width), F32)],
        grads, slope, row, gate, up,
        flops=8 * cap * devices * width * width,
        vmem=24,
    )

    part = chips // 4

    def both(group):
        at = slice(group * part, (group + 1) * part)
        return own[at] + arrived[at].astype(F32)

    def shift(v, hops):
        to = [(i, (i + 2 * hops * (1 - 2 * (i % 2))) % devices) for i in range(devices)]
        return lax.ppermute(v.astype(BF16), "hidden", to).astype(F32)

    passed = shift(both(2), 1)
    near = both(0) + shift(both(1), -1) + shift(both(3) + passed, 1)

    along = 1 + 2 * (lax.axis_index("hidden") % 2)

    def piece(apart):
        return lax.dynamic_index_in_dim(near, (lax.axis_index("hidden") // 8 + apart) % part, 0, keepdims=False)

    passed = shift(piece(2), 4)
    total = piece(0) + shift(piece(4 - along), -4) + shift(piece(along) + passed, 4)
    slot_grad = total.astype(BF16)
    outgoing = mm(packer, slot_grad).astype(BF16)
    arrived = lax.all_to_all(outgoing.reshape(experts, SLOT, width), "expert", 0, 0, tiled=True)
    return mm(sender, arrived.reshape(slots, width)).astype(BF16)


def solution(mesh):
    in_specs = (
        P("expert", "hidden"),
        P("expert", "hidden"),
        P(),
        P("expert", None, "hidden"),
        P("expert", None, "hidden"),
        P("expert", "hidden", None),
        P(),
    )
    out_specs = P("expert", "hidden")
    return jax.shard_map(body, mesh=mesh, in_specs=in_specs, out_specs=out_specs, check_vma=False)
```

```python
import jax
import jax.numpy as jnp
from jax import lax
from jax.experimental import pallas as pl
from jax.experimental.pallas import tpu as pltpu
from jax.sharding import PartitionSpec as P

F32 = jnp.float32
BF16 = jnp.bfloat16
SLOT = 16
LAST = (((1,), (1,)), ((), ()))
FIRST = (((0,), (0,)), ((), ()))
STEPS = (64, 16, 8, 4, 2, 1)
BASE = 13


def mm(a, b, dims=(((1,), (0,)), ((), ()))):
    return lax.dot_general(a, b, dims, preferred_element_type=F32)


def call(kernel, out, *args, flops=0, vmem=16):
    spec = pl.BlockSpec(memory_space=pltpu.VMEM)
    moved = sum(a.size * a.dtype.itemsize for a in args) + sum(o.size * o.dtype.itemsize for o in out)
    return pl.pallas_call(
        kernel,
        out_shape=list(out),
        in_specs=[spec] * len(args),
        out_specs=[spec] * len(out),
        compiler_params=pltpu.CompilerParams(vmem_limit_bytes=vmem * 1024 * 1024),
        cost_estimate=pl.CostEstimate(flops=flops, bytes_accessed=moved, transcendentals=0),
    )(*args)


def shape(dims, dtype):
    return jax.ShapeDtypeStruct(dims, dtype)


def iota(dims, axis):
    return lax.broadcasted_iota(jnp.int32, dims, axis)


def route_kernel(chosen_ref, both_ref, blocks_ref, sender_ref, packer_ref):
    col = lax.axis_index("expert")
    experts, cap = chosen_ref.shape
    count = both_ref.shape[0]
    slots = experts * SLOT
    token = iota((count, cap), 0) + col * count
    lane = iota((count, experts), 1)
    mask = jnp.zeros((count, experts), F32)
    for e in range(experts):
        hit = jnp.sum((chosen_ref[e : e + 1, :] == token).astype(F32), axis=1, keepdims=True)
        mask = jnp.where(lane == e, hit, mask)
    mask = mask.astype(BF16)
    earlier = (iota((count, count), 0) > iota((count, count), 1)).astype(F32).astype(BF16)
    rank = mm(earlier, mask).astype(BF16)
    spread = (iota((experts, slots), 1) // SLOT == iota((experts, slots), 0)).astype(F32).astype(BF16)
    place = (iota((count, slots), 1) % SLOT).astype(F32)
    sender = jnp.logical_and(mm(mask, spread) > 0.5, mm(rank, spread) == place).astype(F32).astype(BF16)
    sender_ref[...] = sender
    blocks_ref[...] = mm(sender, both_ref[...], FIRST).astype(BF16)
    own = chosen_ref[pl.ds(col, 1), :] // count
    block = iota((slots, cap), 0) // SLOT
    held = jnp.sum((own == block).astype(F32), axis=1, keepdims=True)
    before = jnp.sum((own < block).astype(F32), axis=1, keepdims=True)
    place = (iota((slots, 1), 0) % SLOT).astype(F32)
    row = jnp.where(place < held, before + place, -1.0)
    packer_ref[...] = (row == iota((slots, cap), 1).astype(F32)).astype(F32).astype(BF16)


def scale_up(rows):
    top = jnp.max(jnp.max(jnp.abs(rows), axis=1, keepdims=True), axis=0, keepdims=True)
    power = jnp.zeros_like(top)
    factor = jnp.full_like(top, 2.0**BASE)
    for step in STEPS:
        small = top <= 2.0 ** (2 - step)
        top = jnp.where(small, top * 2.0**step, top)
        factor = jnp.where(small, factor * 2.0**step, factor)
        power = jnp.where(small, power + step, power)
    return rows * factor, power


def pack_kernel(arrived_ref, packer_ref, out_ref):
    cap = packer_ref.shape[1]
    half = arrived_ref.shape[1] // 2
    rows = mm(packer_ref[...], arrived_ref[...], FIRST)
    for part in range(2):
        lanes = slice(part * half, (part + 1) * half)
        scaled, power = scale_up(rows[:, lanes])
        out_ref[:cap, lanes] = scaled.astype(BF16)
        out_ref[cap:, lanes] = jnp.broadcast_to(power, (out_ref.shape[0] - cap, half)).astype(BF16)


def expert_kernel(x_ref, gate_ref, up_ref, down_ref, router_ref, sib_ref, grads_ref, slope_ref, row_ref):
    col = lax.axis_index("expert")
    hidden = lax.axis_index("hidden")
    core = hidden % 2
    chips = x_ref.shape[0] // 2
    rows = x_ref.shape[1]
    width = gate_ref.shape[1]
    picks = iota(router_ref.shape, 0) == col
    router = jnp.sum(jnp.where(picks, router_ref[...].astype(F32), 0.0), axis=0, keepdims=True)
    row_ref[...] = router

    def at(j):
        return slice(2 * j * width, 2 * (j + 1) * width)

    pre = jnp.zeros((rows, 2 * width), F32)
    back = jnp.zeros((rows, width), F32)
    logit = jnp.zeros((rows, width), F32)
    for j in range(chips):
        x = jnp.concatenate([x_ref[2 * j, :, :width], x_ref[2 * j + 1, :, :width]], axis=1)
        u = jnp.concatenate([x_ref[2 * j, :, width:], x_ref[2 * j + 1, :, width:]], axis=1)
        pre += mm(x, jnp.concatenate([gate_ref[at(j), :], up_ref[at(j), :]], axis=1))
        back += mm(u, down_ref[:, at(j)], LAST)
        logged = x.astype(F32) * router[:, at(j)]
        logit += logged[:, :width] + logged[:, width:]
    logit = jnp.sum(logit, axis=1, keepdims=True)
    weight = 1.0 / (1.0 + jnp.exp(-logit))
    gate_pre, up_pre = pre[:, :width], pre[:, width:]
    sig = 1.0 / (1.0 + jnp.exp(-gate_pre))
    act = (gate_pre * sig * up_pre).astype(BF16)
    score = jnp.sum(back * act.astype(F32), axis=1, keepdims=True)
    scaled = weight * back
    d_up = (scaled * gate_pre * sig).astype(BF16)
    d_gate = (scaled * up_pre * sig * (1.0 + gate_pre * (1.0 - sig))).astype(BF16)
    grads = jnp.concatenate([d_gate, d_up], axis=1)
    slope = score * (weight * (1.0 - weight))

    grads_ref[...] = grads
    slope_ref[...] = jnp.broadcast_to(slope, slope_ref.shape)
    core_terms(chips, 1 - core, grads, slope, gate_ref, up_ref, row_ref, sib_ref)


def core_terms(chips, core, grads, slope, gate_ref, up_ref, row_ref, out_ref):
    chip = lax.axis_index("hidden") // 2
    width = gate_ref.shape[1]
    part = chips // 4
    along = 1 + 2 * core
    for group, apart in enumerate((0, 4 - along, 2, along)):

        def features(r):
            target = 4 * r + (chip + apart) % 4
            return pl.ds(pl.multiple_of((2 * target + core) * width, width), width)

        for first in range(0, part, 2):
            some = range(first, min(first + 2, part))
            side = [jnp.concatenate([gate_ref[features(r), :], up_ref[features(r), :]], axis=1) for r in some]
            terms = mm(grads, jnp.concatenate(side, axis=0), LAST)
            for i, r in enumerate(some):
                out = terms[:, i * width : (i + 1) * width] + slope * row_ref[:, features(r)]
                out_ref[group * part + r] = out.astype(out_ref.dtype)


def terms_kernel(grads_ref, slope_ref, row_ref, gate_ref, up_ref, own_ref):
    core = lax.axis_index("hidden") % 2
    chips = gate_ref.shape[0] // (2 * gate_ref.shape[1])
    core_terms(chips, core, grads_ref[...], slope_ref[:, :1], gate_ref, up_ref, row_ref, own_ref)


def body(tokens, upstream, router, w_gate, w_up, w_down, chosen):
    experts = lax.axis_size("expert")
    devices = lax.axis_size("hidden")
    chips = devices // 2
    count, width = tokens.shape
    cap = chosen.shape[1]
    slots = experts * SLOT

    blocks, sender, packer = call(
        route_kernel,
        [shape((slots, 2 * width), BF16), shape((count, slots), BF16), shape((slots, cap), BF16)],
        chosen, jnp.concatenate([tokens, upstream], axis=1),
    )
    arrived = lax.all_to_all(blocks.reshape(experts, SLOT, 2 * width), "expert", 0, 0, tiled=True)
    (rows,) = call(pack_kernel, [shape((cap + 16, 2 * width), BF16)], arrived.reshape(slots, 2 * width), packer)
    full = lax.all_gather(rows.astype(jnp.float16), "hidden", axis=0)
    undo = jnp.exp2(-(full[:, cap : cap + 1, :].astype(F32) + BASE))
    picked = (full[:, :cap, :].astype(F32) * undo).astype(BF16)

    gate, up = w_gate[0], w_up[0]
    sibling, grads, slope, row = call(
        expert_kernel,
        [
            shape((chips, cap, width), BF16), shape((cap, 2 * width), BF16), shape((cap, width), F32),
            shape((1, devices * width), F32),
        ],
        picked, gate, up, w_down[0], router.T,
        flops=8 * cap * devices * width * width,
        vmem=24,
    )
    arrived = lax.ppermute(sibling, "hidden", [(i, i ^ 1) for i in range(devices)])
    (own,) = call(
        terms_kernel,
        [shape((chips, cap, width), F32)],
        grads, slope, row, gate, up,
        flops=8 * cap * devices * width * width,
        vmem=24,
    )

    part = chips // 4

    def both(group):
        at = slice(group * part, (group + 1) * part)
        return own[at] + arrived[at].astype(F32)

    def shift(v, hops):
        to = [(i, (i + 2 * hops * (1 - 2 * (i % 2))) % devices) for i in range(devices)]
        return lax.ppermute(v.astype(BF16), "hidden", to).astype(F32)

    passed = shift(both(2), 1)
    near = (both(0) + shift(both(1), -1) + shift(both(3) + passed, 1)).astype(BF16)
    groups = [[c + 2 * q + 8 * r for r in range(part)] for q in range(4) for c in range(2)]
    parts = lax.all_to_all(near, "hidden", 0, 0, tiled=True, axis_index_groups=groups)
    slot_grad = jnp.sum(parts.astype(F32), axis=0).astype(BF16)
    outgoing = mm(packer, slot_grad).astype(BF16)
    arrived = lax.all_to_all(outgoing.reshape(experts, SLOT, width), "expert", 0, 0, tiled=True)
    return mm(sender, arrived.reshape(slots, width)).astype(BF16)


def solution(mesh):
    in_specs = (
        P("expert", "hidden"),
        P("expert", "hidden"),
        P(),
        P("expert", None, "hidden"),
        P("expert", None, "hidden"),
        P("expert", "hidden", None),
        P(),
    )
    out_specs = P("expert", "hidden")
    return jax.shard_map(body, mesh=mesh, in_specs=in_specs, out_specs=out_specs, check_vma=False)
```
